32 devices in a mesh: fields: 2 (over y), row: 4 (over z), col: 4 (over x, core).
Axes of the slice: x: 2, y: 2, z: 4, core: 2. Of those that a mesh axis runs over, the one named last changes fastest.
Arguments:
- root_inverse: bfloat16 [8192, 4096], P(('fields', 'row'), 'col'), parts along dimension 0, as said below
- child_inverse: bfloat16 [4096, 2048], P(('fields', 'row'), 'col'), parts along dimension 0, as said below
- panel: bfloat16 [8192, 2048], P(('fields', 'row'), 'col'), parts along dimension 0, may hold values from -0.09375 to 0.09375
- structure: int32 [64], P(('fields', 'row')), parts along dimension 0, may hold values 0 or 1
Outputs:
- sigma_root: bfloat16 [8192, 4096], P(('fields', 'row'), 'col'), parts along dimension 0
- sigma_cross: bfloat16 [8192, 2048], P(('fields', 'row'), 'col'), parts along dimension 0
- sigma_child: float32 [4096, 2048], P(('fields', 'row'), 'col'), parts along dimension 0
The draws below stay inside these ranges and needn't reach their ends.
There are 2 independent parts, one for each index of `fields`. The reference program is written for one: setup_inputs(seed, part) draws one part's arguments, and reference() takes and returns one part's arrays. A program takes and returns all parts, laid end to end along the dimension named above; each array names one. Nothing has to cross between parts.
Inputs may be any that keep to these rules, and one draw needn't show every extreme that they name: `root_inverse`: lower triangular with a positive diagonal. `child_inverse`: lower triangular with a positive diagonal. 1 marks a block row of 128 root rows in the child's structure.
All inputs are finite; a program needn't handle non-finite values.
Results may differ from the reference program's by a relative error of at most 0.008.
Values may be sent and summed in bfloat16 or wider, within the bound.
No kernel may reach another device: no remote copies, remote signals or barrier semaphores. Data moves between devices by JAX's collectives and lax.ppermute only.
A program may use at most 128 MiB of HBM per device.

```python
import jax
import jax.numpy as jnp
from jax import lax

W1 = 4096
W2 = 2048
BLOCK = 128
NBLK = 32


def triangle(entries, diagonal):
    order = diagonal.shape[0]
    positions = jnp.arange(order)
    below = positions[:, None] > positions[None, :]
    lower = jnp.where(below, entries * order ** (-0.5), jnp.zeros_like(entries))
    return (lower + jnp.diag(diagonal)).astype(jnp.bfloat16)


def draw_root_inverse(key, part):
    key = jax.random.fold_in(key, 1)
    entry_key, diag_key = jax.random.split(key)
    entries = jax.random.normal(entry_key, (W1, W1), jnp.float32)
    diagonal = jax.random.uniform(diag_key, (W1,), jnp.float32, 0.6, 1.4)
    return triangle(entries, diagonal)


def draw_child_inverse(key, part):
    key = jax.random.fold_in(key, 2)
    entry_key, diag_key = jax.random.split(key)
    entries = jax.random.normal(entry_key, (W2, W2), jnp.float32)
    diagonal = jax.random.uniform(diag_key, (W2,), jnp.float32, 0.6, 1.4)
    return triangle(entries, diagonal)


def touch_ends(drawn, stream_key, least, high):
    longest = drawn.shape.index(max(drawn.shape))
    spots = []
    for shift in (0, 1):
        where = [jax.random.randint(jax.random.fold_in(stream_key, axis), (), 0, length) for axis, length in enumerate(drawn.shape)]
        where[longest] = (where[longest] + shift) % drawn.shape[longest]
        spots.append(tuple(where))
    return drawn.at[spots[0]].set(least).at[spots[1]].set(high)


def block_scale(own_key, extent, shards, least, largest):
    def one(axis_at, parts):
        heights = jax.random.uniform(jax.random.fold_in(jax.random.fold_in(own_key, 6), axis_at), (parts,), jnp.float32, least / len(shards), largest / len(shards))
        return jnp.repeat(jnp.exp(heights), extent[axis_at] // parts).reshape((-1,) + (1,) * (len(extent) - axis_at - 1))

    factor_of = one(*shards[0])
    for cut in shards[1:]:
        factor_of = factor_of * one(*cut)
    return factor_of


def scatter_about(own_key, dims, scale, most, shards=(), kind=jnp.bfloat16):
    values = jax.random.normal(own_key, dims, jnp.float32) * scale
    if len(shards) > 0:
        values = block_scale(own_key, dims, shards, -0.22, 0.18) * values
    return jnp.clip(values, min=-most, max=most).astype(kind)


def setup_inputs(seed: int = 0, part: int = 0) -> dict:
    seeds = jax.random.split(jax.random.key(seed), 5)
    own_keys = jax.random.split(jax.random.fold_in(seeds[4], part), 5)
    return {
        "root_inverse": draw_root_inverse(jax.random.fold_in(jax.random.fold_in(seeds[4], part), 71), part),
        "child_inverse": draw_child_inverse(jax.random.fold_in(jax.random.fold_in(seeds[4], part), 71), part),
        "panel": scatter_about(own_keys[2], (W1, W2), W1 ** -0.5, 0.09375, ((0, 4), (1, 4))),
        "structure": touch_ends((jax.random.randint(own_keys[3], (NBLK,), 0, 2) < 1).astype(jnp.int32), jax.random.fold_in(own_keys[3], 1), 0, 1),
    }


def inner_dot(left_part, right_part):
    return lax.dot_general(left_part, right_part, (((0,), (0,)), ((), ())), preferred_element_type=jnp.float32)


def reference(root_inverse, child_inverse, panel, structure):
    kept_rows = jnp.repeat(structure, BLOCK)[:, None] > 0
    panel_kept = jnp.where(kept_rows, panel, jnp.zeros_like(panel))
    sigma_root = inner_dot(root_inverse, root_inverse).astype(jnp.bfloat16)
    cross_sum = jnp.dot(sigma_root, panel_kept, preferred_element_type=jnp.float32)
    sigma_cross = jnp.where(kept_rows, -cross_sum, jnp.zeros_like(cross_sum)).astype(jnp.bfloat16)
    sigma_child = inner_dot(child_inverse, child_inverse) - inner_dot(panel_kept, sigma_cross)
    return sigma_root, sigma_cross, sigma_child
```

```python
import jax
import jax.numpy as jnp
from jax import lax
from jax.sharding import PartitionSpec as P

BLOCK = 128
AXES = ("fields", "row", "col")
BF16 = jnp.bfloat16
F32 = jnp.float32


def inner_dot(left_part, right_part):
    return lax.dot_general(
        left_part, right_part, (((0,), (0,)), ((), ())), preferred_element_type=F32
    )


def mask_panel(panel, structure):
    kept_rows = jnp.repeat(structure, BLOCK)[:, None] > 0
    return kept_rows, jnp.where(kept_rows, panel, jnp.zeros_like(panel))


def gather_plan(root_inverse, child_inverse, panel, structure):
    kept_rows, panel_kept = mask_panel(panel, structure)
    root_full, child_rows, panel_full = (
        lax.all_gather(root_inverse, "col", axis=1, tiled=True),
        lax.all_gather(child_inverse, "col", axis=1, tiled=True),
        lax.all_gather(panel_kept, "col", axis=1, tiled=True),
    )
    root_sum = lax.psum_scatter(
        inner_dot(root_full, root_inverse), "row", scatter_dimension=0, tiled=True
    )
    sigma_root = root_sum.astype(BF16)
    sigma_rows = lax.all_gather(sigma_root, "col", axis=1, tiled=True)
    cross_sum = jnp.dot(
        sigma_rows,
        lax.all_gather(panel_kept, "row", axis=0, tiled=True),
        preferred_element_type=F32,
    )
    sigma_cross = jnp.where(kept_rows, -cross_sum, jnp.zeros_like(cross_sum)).astype(BF16)
    sigma_child = lax.psum_scatter(
        (inner_dot(child_rows, child_inverse) - inner_dot(panel_full, sigma_cross)).astype(BF16),
        "row",
        scatter_dimension=0,
        tiled=True,
    ).astype(F32)
    return (sigma_root, sigma_cross, sigma_child)


def square_plan(fields):
    n = 4

    def move(x, target):
        pairs = []
        for f in range(fields):
            for r in range(n):
                for c in range(n):
                    to = target(r, c)
                    if to is not None and 0 <= to[0] < n:
                        pairs.append(((f * n + r) * n + c, (f * n + to[0]) * n + to[1]))
        return lax.ppermute(x, AXES, pairs)

    def in_row(x, c, nonzero):
        own = x
        across = move(x, lambda r, c: (r, c ^ 2) if nonzero(r, c) else None)
        beside = move(x, lambda r, c: (r, c ^ 1) if nonzero(r, c) else None)
        both = move(across, lambda r, c: (r, c ^ 1) if nonzero(r, c ^ 2) else None)
        h, w = x.shape
        full = jnp.zeros((h, n * w), x.dtype)
        for m, part in enumerate((own, beside, across, both)):
            full = lax.dynamic_update_slice(full, part, (0, (c ^ m) * w))
        return full

    def on_device(root_inverse, child_inverse, panel, structure):
        r, c = lax.axis_index("row"), lax.axis_index("col")
        kept_rows, panel_kept = mask_panel(panel, structure)
        h, w = panel.shape
        lower = lambda r, c: c <= r

        panel_all = jnp.zeros((n * h, w), BF16)
        panels = [panel_kept] + [
            move(panel_kept, lambda r, c, s=s: (r + s, c)) for s in (1, 2, 3)
        ]
        for s in range(n):
            panel_all = lax.dynamic_update_slice(panel_all, panels[s], (((r - s) % n) * h, 0))
        root_row = in_row(root_inverse, c, lower)
        below = [root_inverse] + [
            move(
                root_inverse,
                lambda r, c, s=s: (r - s, c) if c <= r and not (r == s and c == 1) else None,
            )
            for s in (1, 2, 3)
        ]

        t = jnp.dot(root_row, panel_all, preferred_element_type=F32).astype(BF16)
        child_row = in_row(child_inverse, c, lower)
        t_row = in_row(t, c, lambda r, c: True)
        cross = inner_dot(root_row, t).astype(BF16)

        block = lambda x, i, size: lax.dynamic_slice_in_dim(x, i * size, size, 0)
        near = move(block(cross, r ^ 1, h), lambda r, c: (r ^ 1, c) if r % 2 else None)
        far = move(block(cross, r ^ 3, h), lambda r, c: (r ^ 1, c) if r >= 2 else None)
        onward = block(cross, r ^ 2, h) + far
        last = move(onward, lambda r, c: (r - 2, c))
        cross_sum = block(cross, r, h).astype(F32) + near.astype(F32) + last.astype(F32)
        sigma_cross = jnp.where(kept_rows, -cross_sum, jnp.zeros_like(cross_sum)).astype(BF16)

        child = (inner_dot(t_row, t) + inner_dot(child_row, child_inverse)).astype(BF16)
        near = move(block(child, r ^ 1, w), lambda r, c: (r ^ 1, c))
        far = move(block(child, r ^ 3, w), lambda r, c: (r ^ 1, c))
        last = move(block(child, r ^ 2, w) + far, lambda r, c: (r ^ 2, c))
        sigma_child = block(child, r, w).astype(F32) + near.astype(F32) + last.astype(F32)

        root_sum = inner_dot(lax.dynamic_slice_in_dim(root_row, r * h, h, 1), root_inverse)
        for s in (1, 2, 3):
            across = move(
                below[s], lambda r, c, s=s: (r, c ^ 2) if r == c and 2 <= r + s < n else None
            )
            have = jnp.where(c == r, below[s], across)
            beside = move(
                have, lambda r, c, s=s: (r, c ^ 1) if r in (c, c ^ 2) and r + s < n else None
            )
            left = jnp.where((c == r) | (c == (r ^ 2)), have, beside)
            root_sum = root_sum + inner_dot(left, below[s])
        sigma_root = root_sum.astype(BF16)
        mirror = move(sigma_root, lambda r, c: (0, 1) if (r, c) == (1, 0) else None)
        sigma_root = jnp.where((r == 0) & (c == 1), mirror.T, sigma_root)
        return (sigma_root, sigma_cross, sigma_child)

    return on_device


def solution(mesh):
    square = mesh.shape["row"] == 4 and mesh.shape["col"] == 4
    spec = P(("fields", "row"), "col")
    return jax.shard_map(
        square_plan(mesh.shape["fields"]) if square else gather_plan,
        mesh=mesh,
        in_specs=(spec, spec, spec, P(("fields", "row"))),
        out_specs=(spec, spec, spec),
        check_vma=False,
    )
```

```python
import jax
import jax.numpy as jnp
from jax import lax
from jax.experimental import pallas as pl
from jax.sharding import PartitionSpec as P

BLOCK = 128
AXES = ("fields", "row", "col")
BF16 = jnp.bfloat16
F32 = jnp.float32


def inner_dot(left_part, right_part):
    return lax.dot_general(
        left_part, right_part, (((0,), (0,)), ((), ())), preferred_element_type=F32
    )


def mask_panel(panel, structure):
    kept_rows = jnp.repeat(structure, BLOCK)[:, None] > 0
    return kept_rows, jnp.where(kept_rows, panel, jnp.zeros_like(panel))


def gather_plan(root_inverse, child_inverse, panel, structure):
    kept_rows, panel_kept = mask_panel(panel, structure)
    root_full, child_rows, panel_full = (
        lax.all_gather(root_inverse, "col", axis=1, tiled=True),
        lax.all_gather(child_inverse, "col", axis=1, tiled=True),
        lax.all_gather(panel_kept, "col", axis=1, tiled=True),
    )
    root_sum = lax.psum_scatter(
        inner_dot(root_full, root_inverse), "row", scatter_dimension=0, tiled=True
    )
    sigma_root = root_sum.astype(BF16)
    sigma_rows = lax.all_gather(sigma_root, "col", axis=1, tiled=True)
    cross_sum = jnp.dot(
        sigma_rows,
        lax.all_gather(panel_kept, "row", axis=0, tiled=True),
        preferred_element_type=F32,
    )
    sigma_cross = jnp.where(kept_rows, -cross_sum, jnp.zeros_like(cross_sum)).astype(BF16)
    sigma_child = lax.psum_scatter(
        (inner_dot(child_rows, child_inverse) - inner_dot(panel_full, sigma_cross)).astype(BF16),
        "row",
        scatter_dimension=0,
        tiled=True,
    ).astype(F32)
    return (sigma_root, sigma_cross, sigma_child)


def square_plan(fields):
    n = 4

    def move(x, target):
        pairs = []
        for f in range(fields):
            for r in range(n):
                for c in range(n):
                    to = target(r, c)
                    if to is not None and 0 <= to[0] < n:
                        pairs.append(((f * n + r) * n + c, (f * n + to[0]) * n + to[1]))
        return lax.ppermute(x, AXES, pairs)

    def together(*arrays, earlier=()):
        k = len(arrays)
        anywhere = pl.BlockSpec(memory_space=pl.ANY)
        return pl.pallas_call(
            lambda *refs: None,
            out_shape=[jax.ShapeDtypeStruct(x.shape, x.dtype) for x in arrays],
            in_specs=[anywhere] * (k + len(earlier)),
            out_specs=[anywhere] * k,
            input_output_aliases={i: i for i in range(k)},
        )(*arrays, *earlier)

    def on_device(root_inverse, child_inverse, panel, structure):
        r, c = lax.axis_index("row"), lax.axis_index("col")
        kept_rows, panel_kept = mask_panel(panel, structure)
        h, w = panel.shape
        lower = lambda r, c: c <= r
        columns = lambda x, i, size: lax.dynamic_slice_in_dim(x, i * size, size, 1)

        def r_after(*earlier):
            return together(jnp.full((8, 128), r, jnp.int32), earlier=earlier)[0][0, 0]

        def up(x, s):
            return move(x, lambda r, c: (r + 1, c) if r >= s - 1 else None)

        def down(x, s):
            def target(r, c):
                k = r + s - 1
                return (r - 1, c) if k < n and c <= k and (r, c) != (1, 1) else None

            return move(x, target)

        child_row = lax.all_gather(child_inverse, "col", axis=1, tiled=True)
        panel_1 = up(panel_kept, 1)
        root_across = move(root_inverse, lambda r, c: (r, c ^ 2) if lower(r, c) else None)
        below_1 = down(root_inverse, 1)
        root_beside = move(root_inverse, lambda r, c: (r, c ^ 1) if lower(r, c) else None)
        (panel_1,) = together(panel_1, earlier=(root_beside,))
        panel_2 = up(panel_1, 2)
        root_row = jnp.zeros((h, n * h), BF16)
        for m, block in enumerate((root_inverse, root_beside)):
            root_row = lax.dynamic_update_slice(root_row, block, (0, (c ^ m) * h))
        panel_2, below_1, root_across, root_row = together(
            panel_2, below_1, root_across, root_row
        )
        panel_3 = up(panel_2, 3)
        half = h // 2
        below_2a = down(below_1[:half], 2)
        root_both = move(root_across, lambda r, c: (r, c ^ 1) if lower(r, c ^ 2) else None)
        across_1 = move(below_1, lambda r, c: (r, c ^ 2) if r == c and r in (1, 2) else None)

        panel_3, below_2a, across_1 = together(panel_3, below_2a, across_1)
        for m, block in ((2, root_across), (3, root_both)):
            root_row = lax.dynamic_update_slice(root_row, block, (0, (c ^ m) * h))
        t = jnp.zeros((h, w), F32)
        for s, block in enumerate((panel_kept, panel_1, panel_2, panel_3)):
            t = t + jnp.dot(columns(root_row, (r - s) % n, h), block, preferred_element_type=F32)
        t = t.astype(BF16)
        t_row = lax.all_gather(t, "col", axis=1, tiled=True)
        below_2b = down(below_1[half:], 2)
        below_3a = down(below_2a, 3)

        part = lambda i: inner_dot(columns(root_row, i, h), t)
        far_part = part(r ^ 3).astype(BF16)
        far = move(far_part, lambda r, c: (r ^ 1, c) if r >= 2 else None)
        near_part = part(r_after(far_part) ^ 1).astype(BF16)
        below_2b, below_3a = together(below_2b, below_3a, earlier=(near_part, far))
        below_2 = jnp.concatenate((below_2a, below_2b), 0)
        below_3b = down(below_2b, 3)
        r_cross = r_after(near_part, below_2b)
        onward = (part(r_cross ^ 2) + far.astype(F32)).astype(BF16)
        near = move(near_part, lambda r, c: (r ^ 1, c) if r % 2 else None)
        last = move(onward, lambda r, c: (r - 2, c))
        own = part(r_after(onward))
        cross_sum = own + near.astype(F32) + last.astype(F32)
        sigma_cross = jnp.where(kept_rows, -cross_sum, jnp.zeros_like(cross_sum)).astype(BF16)

        part = lambda i: inner_dot(columns(t_row, i, w), t) + inner_dot(
            columns(child_row, i, w), child_inverse
        )
        child_far = part(r_after(onward) ^ 3).astype(BF16)
        far = move(child_far, lambda r, c: (r ^ 1, c))
        child_near = part(r_after(child_far) ^ 1).astype(BF16)
        child_near_in = move(child_near, lambda r, c: (r ^ 1, c))
        r_child = r_after(child_near, far, near, below_3b)
        child_onward = (part(r_child ^ 2) + far.astype(F32)).astype(BF16)
        last = move(child_onward, lambda r, c: (r ^ 2, c))
        sigma_child = part(r_child) + child_near_in.astype(F32) + last.astype(F32)

        root_sum = inner_dot(columns(root_row, r_cross, h), root_inverse)
        (below_3a,) = together(below_3a, earlier=(child_onward,))
        below_3 = jnp.concatenate((below_3a, below_3b), 0)
        r_root = {1: r_after(onward), 2: r_after(child_near), 3: r_after(child_onward)}
        across = {
            1: across_1,
            2: move(below_2, lambda r, c: (r, c ^ 2) if r == c and r in (0, 1) else None),
            3: move(below_3, lambda r, c: (r, c ^ 2) if r == c == 0 else None),
        }
        for s, held in ((1, below_1), (2, below_2), (3, below_3)):
            have = jnp.where(c == r_root[s], held, across[s])
            beside = move(
                have, lambda r, c, s=s: (r, c ^ 1) if r in (c, c ^ 2) and r + s < n else None
            )
            left = jnp.where((c == r) | (c == (r ^ 2)), have, beside)
            if s == 3:
                mirror = move(
                    root_sum.astype(BF16), lambda r, c: (0, 1) if (r, c) == (1, 0) else None
                )
            root_sum = root_sum + inner_dot(left, held)
        sigma_root = jnp.where((r == 0) & (c == 1), mirror.T, root_sum.astype(BF16))
        return (sigma_root, sigma_cross, sigma_child)

    return on_device


def solution(mesh):
    square = mesh.shape["row"] == 4 and mesh.shape["col"] == 4
    spec = P(("fields", "row"), "col")
    return jax.shard_map(
        square_plan(mesh.shape["fields"]) if square else gather_plan,
        mesh=mesh,
        in_specs=(spec, spec, spec, P(("fields", "row"))),
        out_specs=(spec, spec, spec),
        check_vma=False,
    )
```

```python
import jax
import jax.numpy as jnp
from jax import lax
from jax.experimental import pallas as pl
from jax.experimental.pallas import tpu as pltpu
from jax.sharding import PartitionSpec as P

BLOCK = 128
AXES = ("fields", "row", "col")
BF16 = jnp.bfloat16
F32 = jnp.float32
TILE = 256
N = 4
VMEM_BYTES = 40 * 1024 * 1024


def inner_dot(left_part, right_part):
    return lax.dot_general(
        left_part, right_part, (((0,), (0,)), ((), ())), preferred_element_type=F32
    )


def dot(a, b):
    return jnp.dot(a, b, preferred_element_type=F32)


def mask_panel(panel, structure):
    kept_rows = jnp.repeat(structure, BLOCK)[:, None] > 0
    return kept_rows, jnp.where(kept_rows, panel, jnp.zeros_like(panel))


def gather_plan(root_inverse, child_inverse, panel, structure):
    kept_rows, panel_kept = mask_panel(panel, structure)
    root_full, child_rows, panel_full = (
        lax.all_gather(root_inverse, "col", axis=1, tiled=True),
        lax.all_gather(child_inverse, "col", axis=1, tiled=True),
        lax.all_gather(panel_kept, "col", axis=1, tiled=True),
    )
    root_sum = lax.psum_scatter(
        inner_dot(root_full, root_inverse), "row", scatter_dimension=0, tiled=True
    )
    sigma_root = root_sum.astype(BF16)
    sigma_rows = lax.all_gather(sigma_root, "col", axis=1, tiled=True)
    cross_sum = jnp.dot(
        sigma_rows,
        lax.all_gather(panel_kept, "row", axis=0, tiled=True),
        preferred_element_type=F32,
    )
    sigma_cross = jnp.where(kept_rows, -cross_sum, jnp.zeros_like(cross_sum)).astype(BF16)
    sigma_child = lax.psum_scatter(
        (inner_dot(child_rows, child_inverse) - inner_dot(panel_full, sigma_cross)).astype(BF16),
        "row",
        scatter_dimension=0,
        tiled=True,
    ).astype(F32)
    return (sigma_root, sigma_cross, sigma_child)


def position():
    return lax.axis_index("row"), lax.axis_index("col")


def start(src, dst, sem):
    pltpu.make_async_copy(src, dst, sem).start()


def wait(src, dst, sem):
    pltpu.make_async_copy(src, dst, sem).wait()


def start_picked(refs, index, dst, sem):
    for m, ref in enumerate(refs):

        @pl.when(index == m)
        def _():
            start(ref, dst, sem)


def tile(i):
    return pl.ds(pl.multiple_of(i * TILE, TILE), TILE)


def product_kernel(
    l0, l1, l2, l3, p0, p1, p2, p3, _dep0, _dep1, _in, t_ref, tt_ref, far_ref, _out, rows, panels, acc, row_sems, panel_sems
):
    r, c = position()
    for m, ref in enumerate((l0, l1, l2, l3)):
        j = c ^ m

        @pl.when(j <= r)
        def _():
            start(ref, rows.at[r - j], row_sems.at[r - j])

    for s, ref in enumerate((p0, p1, p2, p3)):

        @pl.when(s <= r)
        def _():
            start(ref, panels.at[s], panel_sems.at[s])

    for s in range(N):

        @pl.when(s <= r)
        def _():
            wait(l0, rows.at[s], row_sems.at[s])
            wait(p0, panels.at[s], panel_sems.at[s])

            @pl.loop(0, acc.shape[0] // TILE)
            def _(i):
                term = dot(rows[s, tile(i), :], panels[s])
                if s > 0:
                    term = term + acc[tile(i), :]
                acc[tile(i), :] = term

    @pl.loop(0, acc.shape[0] // TILE)
    def _(i):
        value = acc[tile(i), :]
        t_ref[tile(i), :] = value.astype(BF16)
        tt_ref[:, tile(i)] = value.T.astype(BF16)

    @pl.when(r >= 2)
    def _():
        slot = r - (r ^ 3)

        @pl.loop(0, tt_ref.shape[0] // TILE)
        def _(i):
            far_ref[tile(i), :] = dot(tt_ref[tile(i), :], rows[slot]).astype(BF16)


def cross_kernel(l0, l1, l2, l3, tt_ref, near_ref, own_ref, blocks, sems):
    r, c = position()
    refs = (l0, l1, l2, l3)

    @pl.when(r % 2 == 1)
    def _():
        start_picked(refs, r ^ 1 ^ c, blocks.at[0], sems.at[0])

    start_picked(refs, r ^ c, blocks.at[1], sems.at[1])

    @pl.when(r % 2 == 1)
    def _():
        wait(l0, blocks.at[0], sems.at[0])

        @pl.loop(0, tt_ref.shape[0] // TILE)
        def _(i):
            near_ref[tile(i), :] = dot(tt_ref[tile(i), :], blocks[0]).astype(BF16)

    wait(l0, blocks.at[1], sems.at[1])

    @pl.loop(0, tt_ref.shape[0] // TILE)
    def _(i):
        own_ref[tile(i), :] = dot(tt_ref[tile(i), :], blocks[1])


def onward_kernel(l0, l1, l2, l3, tt_ref, far_ref, _dep0, _ina, _inb, onward_ref, _outa, _outb, block, sem):
    r, c = position()

    @pl.when(r >= 2)
    def _():
        start_picked((l0, l1, l2, l3), r ^ 2 ^ c, block, sem)
        wait(l0, block, sem)

        @pl.loop(0, tt_ref.shape[0] // TILE)
        def _(i):
            term = dot(tt_ref[tile(i), :], block[...])
            onward_ref[tile(i), :] = (term + far_ref[tile(i), :].astype(F32)).astype(BF16)


def child_kernel(tt_ref, t_row_ref, child_ref, child_row_ref, _dep, _in, out_ref, _out, child_t):
    w = child_ref.shape[1]
    child_t[...] = child_ref[...].astype(F32).T.astype(BF16)
    for i in range(N):
        columns = slice(i * w, (i + 1) * w)

        @pl.loop(0, w // TILE)
        def _(j):
            term = dot(tt_ref[tile(j), :], t_row_ref[:, columns])
            term = term + dot(child_t[tile(j), :], child_row_ref[:, columns])
            out_ref[i, tile(j), :] = term.astype(BF16)


def add_root(s, r, c, left, held, acc, first):
    @pl.when((r + s < N) & (c <= r + s))
    def _():
        @pl.loop(0, acc.shape[0] // TILE)
        def _(i):
            term = inner_dot(left[:, tile(i)], held[...])
            if not first:
                term = term + acc[tile(i), :]
            acc[tile(i), :] = term


def root_kernel(l0, l1, l2, l3, h1, x1, h2, x2, b12, _dep, acc_ref, left, held, left_sems, held_sems):
    r, c = position()
    start_picked((l0, l1, l2, l3), r ^ c, left.at[0], left_sems.at[0])
    start(l0, held.at[0], held_sems.at[0])
    b1, b2 = b12.at[: h1.shape[0]], b12.at[h1.shape[0] :]
    for s, refs in ((1, (h1, x1, b1)), (2, (h2, x2, b2))):
        start_picked(refs, source(r, c), left.at[s], left_sems.at[s])
        start(refs[0], held.at[s], held_sems.at[s])
    acc_ref[...] = jnp.zeros_like(acc_ref)
    for s in range(3):
        wait(l0, left.at[s], left_sems.at[s])
        wait(l0, held.at[s], held_sems.at[s])
        add_root(s, r, c, left.at[s], held.at[s], acc_ref, False)


def source(r, c):
    return jnp.where(c == r, 0, jnp.where(c == (r ^ 2), 1, 2))


def root_end_kernel(acc_ref, h3, x3, b3, out_ref, left, held, sems):
    r, c = position()

    @pl.when(r == 0)
    def _():
        start_picked((h3, x3, b3), source(r, c), left, sems.at[0])
        start(h3, held, sems.at[1])
        wait(h3, left, sems.at[0])
        wait(h3, held, sems.at[1])

        @pl.loop(0, left.shape[0] // TILE)
        def _(i):
            term = inner_dot(left[:, tile(i)], held[...])
            out_ref[tile(i), :] = (term + acc_ref[tile(i), :]).astype(BF16)

    @pl.when(r != 0)
    def _():
        out_ref[...] = acc_ref[...].astype(BF16)


def cross_end_kernel(structure, own_ref, near_ref, last_ref, out_ref):
    for b in range(own_ref.shape[1] // BLOCK):
        rows = slice(b * BLOCK, (b + 1) * BLOCK)
        total = own_ref[:, rows] + near_ref[:, rows].astype(F32) + last_ref[:, rows].astype(F32)
        kept = structure[b] > 0
        out_ref[rows, :] = jnp.where(kept, -total.T, jnp.zeros_like(total.T)).astype(BF16)


def child_end_kernel(sum_ref, _dep, out_ref):
    out_ref[...] = sum_ref[...].astype(F32).T


ANY = pl.BlockSpec(memory_space=pl.ANY)
VMEM = pl.BlockSpec(memory_space=pltpu.VMEM)
SMEM = pl.BlockSpec(memory_space=pltpu.SMEM)


def local_call(kernel, in_specs, outs, scratch, *args, gated=0):
    first = len(args) - gated
    outs = outs + [jax.ShapeDtypeStruct(x.shape, x.dtype) for x in args[first:]]
    return pl.pallas_call(
        kernel,
        out_shape=outs,
        in_specs=in_specs + [ANY] * (len(args) - len(in_specs)),
        out_specs=[VMEM] * (len(outs) - gated) + [ANY] * gated,
        scratch_shapes=scratch,
        input_output_aliases={first + i: len(outs) - gated + i for i in range(gated)},
        compiler_params=pltpu.CompilerParams(vmem_limit_bytes=VMEM_BYTES),
        cost_estimate=pl.CostEstimate(flops=1, bytes_accessed=1, transcendentals=0),
    )(*args)


def together(*arrays, earlier=()):
    k = len(arrays)
    return pl.pallas_call(
        lambda *refs: None,
        out_shape=[jax.ShapeDtypeStruct(x.shape, x.dtype) for x in arrays],
        in_specs=[ANY] * (k + len(earlier)),
        out_specs=[ANY] * k,
        input_output_aliases={i: i for i in range(k)},
    )(*arrays, *earlier)


def square_plan(fields):
    n = N

    def move(x, target):
        pairs = []
        for f in range(fields):
            for r in range(n):
                for c in range(n):
                    to = target(r, c)
                    if to is not None and 0 <= to[0] < n:
                        pairs.append(((f * n + r) * n + c, (f * n + to[0]) * n + to[1]))
        return lax.ppermute(x, AXES, pairs)

    def up(x, s):
        return move(x, lambda r, c: (r + 1, c) if r >= s - 1 else None)

    def down(x, s):
        def target(r, c):
            k = r + s - 1
            return (r - 1, c) if k < n and c <= k else None

        return move(x, target)

    def on_device(root_inverse, child_inverse, panel, structure):
        kept_rows, panel_kept = mask_panel(panel, structure)
        h, w = panel.shape
        half = h // 2
        lower = lambda r, c: c <= r
        shape = jax.ShapeDtypeStruct
        dma = pltpu.SemaphoreType.DMA

        child_row = lax.all_gather(child_inverse, "col", axis=1, tiled=True)
        panel_1 = up(panel_kept, 1)
        root_across = move(root_inverse, lambda r, c: (r, c ^ 2) if lower(r, c) else None)
        below_1 = down(root_inverse, 1)
        root_beside = move(root_inverse, lambda r, c: (r, c ^ 1) if lower(r, c) else None)
        panel_2 = up(panel_1, 2)
        (panel_2,) = together(panel_2, earlier=(below_1, root_across, root_beside))
        panel_3 = up(panel_2, 3)
        below_2a = down(below_1[:half], 2)
        root_both = move(root_across, lambda r, c: (r, c ^ 1) if lower(r, c ^ 2) else None)
        across_1 = move(below_1, lambda r, c: (r, c ^ 2) if r == c and r in (1, 2) else None)

        root_row = (root_inverse, root_beside, root_across, root_both)
        panels = (panel_kept, panel_1, panel_2, panel_3)
        t, t_t, far_part, below_1 = local_call(
            product_kernel,
            [ANY] * 10,
            [shape((h, w), BF16), shape((w, h), BF16), shape((w, h), BF16)],
            [
                pltpu.VMEM((n, h, h), BF16),
                pltpu.VMEM((n, h, w), BF16),
                pltpu.VMEM((h, w), F32),
                dma((n,)),
                dma((n,)),
            ],
            *root_row,
            *panels,
            below_2a,
            across_1,
            below_1,
            gated=1,
        )
        t_row = lax.all_gather(t, "col", axis=1, tiled=True)
        far = move(far_part, lambda r, c: (r ^ 1, c) if r >= 2 else None)
        below_2b = down(below_1[half:], 2)

        near_part, own = local_call(
            cross_kernel,
            [ANY] * 4 + [VMEM],
            [shape((w, h), BF16), shape((w, h), F32)],
            [pltpu.VMEM((2, h, h), BF16), dma((2,))],
            *root_row,
            t_t,
        )
        near = move(near_part, lambda r, c: (r ^ 1, c) if r % 2 else None)
        onward, below_2a, below_2b = local_call(
            onward_kernel,
            [ANY] * 4 + [VMEM, VMEM],
            [shape((w, h), BF16)],
            [pltpu.VMEM((h, h), BF16), dma],
            *root_row,
            t_t,
            far,
            near_part,
            below_2a,
            below_2b,
            gated=2,
        )
        last = move(onward, lambda r, c: (r - 2, c))
        below_2 = jnp.concatenate((below_2a, below_2b), 0)
        below_3 = down(below_2, 3)
        across_2 = move(below_2, lambda r, c: (r, c ^ 2) if r == c and r in (0, 1) else None)

        child_parts, across_1 = local_call(
            child_kernel,
            [VMEM] * 4,
            [shape((n, w, w), BF16)],
            [pltpu.VMEM((w, w), BF16)],
            t_t,
            t_row,
            child_inverse,
            child_row,
            onward,
            across_1,
            gated=1,
        )
        child_sum = lax.psum_scatter(child_parts, "row", scatter_dimension=0)

        r, c = lax.axis_index("row"), lax.axis_index("col")
        across_1, below_3 = together(across_1, below_3, earlier=(near, last))
        across_3 = move(below_3, lambda r, c: (r, c ^ 2) if r == c == 0 else None)
        held_12 = jnp.concatenate((below_1, below_2), 0)
        beside_12 = move(
            jnp.where(c == r, held_12, jnp.concatenate((across_1, across_2), 0)),
            lambda r, c: (r, c ^ 1) if r in (c, c ^ 2) and r < 3 else None,
        )
        (root_sum,) = local_call(
            root_kernel,
            [],
            [shape((h, h), F32)],
            [pltpu.VMEM((3, h, h), BF16), pltpu.VMEM((3, h, h), BF16), dma((3,)), dma((3,))],
            *root_row,
            below_1,
            across_1,
            below_2,
            across_2,
            beside_12,
            child_parts,
        )
        (sigma_cross,) = local_call(
            cross_end_kernel,
            [SMEM] + [VMEM] * 3,
            [shape((h, w), BF16)],
            [],
            structure,
            own,
            near,
            last,
        )
        beside_3 = move(
            jnp.where(c == r, below_3, across_3),
            lambda r, c: (r, c ^ 1) if r == 0 and c in (0, 2) else None,
        )
        (sigma_root,) = local_call(
            root_end_kernel,
            [VMEM],
            [shape((h, h), BF16)],
            [pltpu.VMEM((h, h), BF16), pltpu.VMEM((h, h), BF16), dma((2,))],
            root_sum,
            below_3,
            across_3,
            beside_3,
        )
        (sigma_child,) = local_call(
            child_end_kernel,
            [VMEM],
            [shape((w, w), F32)],
            [],
            child_sum,
            sigma_cross,
        )
        return (sigma_root, sigma_cross, sigma_child)

    return on_device


def solution(mesh):
    square = mesh.shape["row"] == N and mesh.shape["col"] == N
    spec = P(("fields", "row"), "col")
    return jax.shard_map(
        square_plan(mesh.shape["fields"]) if square else gather_plan,
        mesh=mesh,
        in_specs=(spec, spec, spec, P(("fields", "row"))),
        out_specs=(spec, spec, spec),
        check_vma=False,
    )
```

```python
import functools

import jax
import jax.numpy as jnp
from jax import lax
from jax.experimental import pallas as pl
from jax.experimental.pallas import tpu as pltpu
from jax.sharding import PartitionSpec as P

BLOCK = 128
AXES = ("fields", "row", "col")
BF16 = jnp.bfloat16
F32 = jnp.float32
TILE = 256
N = 4
VMEM_BYTES = 40 * 1024 * 1024


def inner_dot(left_part, right_part):
    return lax.dot_general(
        left_part, right_part, (((0,), (0,)), ((), ())), preferred_element_type=F32
    )


def dot(a, b):
    return jnp.dot(a, b, preferred_element_type=F32)


def mask_panel(panel, structure):
    kept_rows = jnp.repeat(structure, BLOCK)[:, None] > 0
    return kept_rows, jnp.where(kept_rows, panel, jnp.zeros_like(panel))


def gather_plan(root_inverse, child_inverse, panel, structure):
    kept_rows, panel_kept = mask_panel(panel, structure)
    root_full, child_rows, panel_full = (
        lax.all_gather(root_inverse, "col", axis=1, tiled=True),
        lax.all_gather(child_inverse, "col", axis=1, tiled=True),
        lax.all_gather(panel_kept, "col", axis=1, tiled=True),
    )
    root_sum = lax.psum_scatter(
        inner_dot(root_full, root_inverse), "row", scatter_dimension=0, tiled=True
    )
    sigma_root = root_sum.astype(BF16)
    sigma_rows = lax.all_gather(sigma_root, "col", axis=1, tiled=True)
    cross_sum = jnp.dot(
        sigma_rows,
        lax.all_gather(panel_kept, "row", axis=0, tiled=True),
        preferred_element_type=F32,
    )
    sigma_cross = jnp.where(kept_rows, -cross_sum, jnp.zeros_like(cross_sum)).astype(BF16)
    sigma_child = lax.psum_scatter(
        (inner_dot(child_rows, child_inverse) - inner_dot(panel_full, sigma_cross)).astype(BF16),
        "row",
        scatter_dimension=0,
        tiled=True,
    ).astype(F32)
    return (sigma_root, sigma_cross, sigma_child)


def position():
    return lax.axis_index("row"), lax.axis_index("col")


def start(src, dst, sem):
    pltpu.make_async_copy(src, dst, sem).start()


def wait(src, dst, sem):
    pltpu.make_async_copy(src, dst, sem).wait()


def start_picked(refs, index, dst, sem):
    for m, ref in enumerate(refs):

        @pl.when(index == m)
        def _():
            start(ref, dst, sem)


def tile(i):
    return pl.ds(pl.multiple_of(i * TILE, TILE), TILE)


def far_block(r):
    return jnp.where(r == 1, 0, r ^ 3)


def product_kernel(
    structure, l0, l1, l2, l3, p0, p1, p2, p3, *refs, deps, gated
):
    t_ref, tt_ref, far_ref = refs[deps + gated : deps + gated + 3]
    rows, panels, acc, row_sems, panel_sems = refs[deps + 2 * gated + 3 :]
    r, c = position()
    blocks = panels.shape[1] // BLOCK
    for m, ref in enumerate((l0, l1, l2, l3)):
        j = c ^ m

        @pl.when(j <= r)
        def _():
            start(ref, rows.at[r - j], row_sems.at[r - j])

    for s, ref in enumerate((p0, p1, p2, p3)):

        @pl.when(s <= r)
        def _():
            start(ref, panels.at[s], panel_sems.at[s])

    for s in range(N):

        @pl.when(s <= r)
        def _():
            wait(p0, panels.at[s], panel_sems.at[s])
            for b in range(blocks):

                @pl.when(structure[(r - s) * blocks + b] == 0)
                def _():
                    panels[s, b * BLOCK : (b + 1) * BLOCK, :] = jnp.zeros(
                        (BLOCK, panels.shape[2]), BF16
                    )

            wait(l0, rows.at[s], row_sems.at[s])

            @pl.loop(0, acc.shape[0] // TILE)
            def _(i):
                term = dot(rows[s, tile(i), :], panels[s])
                if s > 0:
                    term = term + acc[tile(i), :]
                acc[tile(i), :] = term

    @pl.loop(0, acc.shape[0] // TILE)
    def _(i):
        value = acc[tile(i), :]
        t_ref[tile(i), :] = value.astype(BF16)
        tt_ref[:, tile(i)] = value.T.astype(BF16)

    @pl.when(r >= 1)
    def _():
        slot = r - far_block(r)

        @pl.loop(0, tt_ref.shape[0] // TILE)
        def _(i):
            far_ref[tile(i), :] = dot(tt_ref[tile(i), :], rows[slot]).astype(BF16)


def cross_kernel(l0, l1, l2, l3, tt_ref, near_ref, own_ref, blocks, sems):
    r, c = position()
    refs = (l0, l1, l2, l3)

    @pl.when(r == 3)
    def _():
        start_picked(refs, r ^ 1 ^ c, blocks.at[0], sems.at[0])

    start_picked(refs, r ^ c, blocks.at[1], sems.at[1])

    @pl.when(r == 3)
    def _():
        wait(l0, blocks.at[0], sems.at[0])

        @pl.loop(0, tt_ref.shape[0] // TILE)
        def _(i):
            near_ref[tile(i), :] = dot(tt_ref[tile(i), :], blocks[0]).astype(BF16)

    wait(l0, blocks.at[1], sems.at[1])

    @pl.loop(0, tt_ref.shape[0] // TILE)
    def _(i):
        own_ref[tile(i), :] = dot(tt_ref[tile(i), :], blocks[1])


def onward_kernel(l0, l1, l2, l3, tt_ref, far_ref, *refs, deps):
    onward_ref, _, block, sem = refs[deps:]
    r, c = position()

    @pl.when(r >= 2)
    def _():
        start_picked((l0, l1, l2, l3), r ^ 2 ^ c, block, sem)
        wait(l0, block, sem)

        @pl.loop(0, tt_ref.shape[0] // TILE)
        def _(i):
            term = dot(tt_ref[tile(i), :], block[...])
            onward_ref[tile(i), :] = (term + far_ref[tile(i), :].astype(F32)).astype(BF16)


def child_kernel(
    tt_ref, t_row_ref, child_ref, child_row_ref, _dep, far_ref, near_ref, onward_ref, own_ref, child_t
):
    r, _ = position()
    w = child_ref.shape[1]
    child_t[...] = child_ref[...].astype(F32).T.astype(BF16)
    for flip, ref in ((3, far_ref), (1, near_ref), (2, onward_ref), (0, own_ref)):
        columns = pl.ds(pl.multiple_of((r ^ flip) * w, w), w)

        @pl.loop(0, w // TILE)
        def _(i):
            term = dot(tt_ref[tile(i), :], t_row_ref[:, columns])
            term = term + dot(child_t[tile(i), :], child_row_ref[:, columns])
            ref[tile(i), :] = term.astype(ref.dtype)


def child_onward_kernel(own_ref, far_ref, _dep0, _dep1, _dep2, out_ref):
    out_ref[...] = (own_ref[...] + far_ref[...].astype(F32)).astype(BF16)


def diagonal_kernel(l0, l1, l2, l3, _dep, acc_ref, left, held, sems):
    r, c = position()

    @pl.when(c <= r)
    def _():
        start_picked((l0, l1, l2, l3), r ^ c, left, sems.at[0])
        start(l0, held, sems.at[1])
        wait(l0, left, sems.at[0])
        wait(l0, held, sems.at[1])

        @pl.loop(0, acc_ref.shape[0] // TILE)
        def _(i):
            acc_ref[tile(i), :] = inner_dot(left[:, tile(i)], held[...])

    @pl.when(c > r)
    def _():
        acc_ref[...] = jnp.zeros_like(acc_ref)


def pick_kernel(h1, h2, h3, x1, x2, x3, _dep, out_ref, sems):
    r, c = position()
    rows = h1.shape[0]
    for refs, holds in (((h1, h2, h3), c == r), ((x1, x2, x3), c == (r ^ 2))):

        @pl.when(holds)
        def _():
            for act in (start, wait):
                for s, ref in enumerate(refs):
                    act(ref, out_ref.at[s * rows : (s + 1) * rows], sems.at[s])


def root_kernel(acc_ref, h1, h2, h3, x1, x2, x3, beside, out_ref, acc, left, held, left_sems, held_sems):
    r, c = position()
    rows = h1.shape[0]
    refs = ((h1, x1), (h2, x2), (h3, x3))
    needed = [(r + s < N) & (c <= r + s) for s in (1, 2, 3)]
    for s, (own, other) in enumerate(refs):

        @pl.when(needed[s])
        def _():
            places = (own, other, beside.at[s * rows : (s + 1) * rows])
            start_picked(places, source(r, c), left.at[s], left_sems.at[s])
            start(own, held.at[s], held_sems.at[s])

    acc[...] = acc_ref[...]
    for s in range(3):

        @pl.when(needed[s])
        def _():
            wait(h1, left.at[s], left_sems.at[s])
            wait(h1, held.at[s], held_sems.at[s])

            @pl.loop(0, acc.shape[0] // TILE)
            def _(i):
                acc[tile(i), :] += inner_dot(left[s, :, tile(i)], held[s])

    out_ref[...] = acc[...].astype(BF16)


def source(r, c):
    return jnp.where(c == r, 0, jnp.where(c == (r ^ 2), 1, 2))


def cross_end_kernel(structure, own_ref, far_ref, near_ref, last_ref, out_ref):
    first = position()[0] == 0
    for b in range(own_ref.shape[1] // BLOCK):
        rows = slice(b * BLOCK, (b + 1) * BLOCK)
        total = own_ref[:, rows] + near_ref[:, rows].astype(F32) + last_ref[:, rows].astype(F32)
        total = total + jnp.where(first, far_ref[:, rows].astype(F32), jnp.zeros_like(total))
        kept = structure[b] > 0
        out_ref[rows, :] = jnp.where(kept, -total.T, jnp.zeros_like(total.T)).astype(BF16)


def child_end_kernel(own_ref, near_ref, last_ref, out_ref):
    total = own_ref[...] + near_ref[...].astype(F32) + last_ref[...].astype(F32)
    out_ref[...] = total.T


ANY = pl.BlockSpec(memory_space=pl.ANY)
VMEM = pl.BlockSpec(memory_space=pltpu.VMEM)
SMEM = pl.BlockSpec(memory_space=pltpu.SMEM)


def local_call(kernel, in_specs, outs, scratch, *args, gated=0, out_specs=None):
    first = len(args) - gated
    outs = outs + [jax.ShapeDtypeStruct(x.shape, x.dtype) for x in args[first:]]
    return pl.pallas_call(
        kernel,
        out_shape=outs,
        in_specs=in_specs + [ANY] * (len(args) - len(in_specs)),
        out_specs=(out_specs or [VMEM] * (len(outs) - gated)) + [ANY] * gated,
        scratch_shapes=scratch,
        input_output_aliases={first + i: len(outs) - gated + i for i in range(gated)},
        compiler_params=pltpu.CompilerParams(vmem_limit_bytes=VMEM_BYTES),
        cost_estimate=pl.CostEstimate(flops=1, bytes_accessed=1, transcendentals=0),
    )(*args)


def together(*arrays, earlier=()):
    k = len(arrays)
    return pl.pallas_call(
        lambda *refs: None,
        out_shape=[jax.ShapeDtypeStruct(x.shape, x.dtype) for x in arrays],
        in_specs=[ANY] * (k + len(earlier)),
        out_specs=[ANY] * k,
        input_output_aliases={i: i for i in range(k)},
    )(*arrays, *earlier)


def square_plan(fields):
    n = N

    def move(x, target):
        pairs = []
        for f in range(fields):
            for r in range(n):
                for c in range(n):
                    to = target(r, c)
                    if to is not None and 0 <= to[0] < n:
                        pairs.append(((f * n + r) * n + c, (f * n + to[0]) * n + to[1]))
        return lax.ppermute(x, AXES, pairs)

    def up(x, s):
        return move(x, lambda r, c: (r + 1, c) if r >= s - 1 else None)

    def down(x, s):
        def target(r, c):
            k = r + s - 1
            return (r - 1, c) if k < n and c <= k else None

        return move(x, target)

    def on_device(root_inverse, child_inverse, panel, structure):
        h, w = panel.shape
        half = h // 2
        lower = lambda r, c: c <= r
        shape = jax.ShapeDtypeStruct
        dma = pltpu.SemaphoreType.DMA
        t_block, child_block = shape((w, h), BF16), shape((w, w), BF16)

        panel_1 = up(panel, 1)
        below_1a = down(root_inverse[:half], 1)
        root_across = move(root_inverse, lambda r, c: (r, c ^ 2) if lower(r, c) else None)
        root_beside = move(root_inverse, lambda r, c: (r, c ^ 1) if lower(r, c) else None)
        structure_all = lax.all_gather(structure, "row", tiled=True)
        child_row = lax.all_gather(child_inverse, "col", axis=1, tiled=True)
        panel_1, lower_half = together(
            panel_1, root_inverse[half:], earlier=(below_1a, root_beside)
        )
        panel_2 = up(panel_1, 2)
        below_1b = down(lower_half, 1)
        below_2a = down(below_1a, 2)
        (panel_2,) = together(panel_2, earlier=(root_across,))
        panel_3 = up(panel_2, 3)
        root_both = move(root_across, lambda r, c: (r, c ^ 1) if lower(r, c ^ 2) else None)
        below_2b = down(below_1b, 2)
        below_1 = jnp.concatenate((below_1a, below_1b), 0)
        across_1 = move(below_1, lambda r, c: (r, c ^ 2) if r == c and r in (1, 2) else None)

        root_row = (root_inverse, root_beside, root_across, root_both)
        panels = (panel, panel_1, panel_2, panel_3)
        t, t_t, far_part, below_2a, below_2b, root_across_late = local_call(
            functools.partial(product_kernel, deps=1, gated=3),
            [SMEM] + [ANY] * 8,
            [shape((h, w), BF16), t_block, t_block],
            [
                pltpu.VMEM((n, h, h), BF16),
                pltpu.VMEM((n, h, w), BF16),
                pltpu.VMEM((h, w), F32),
                dma((n,)),
                dma((n,)),
            ],
            structure_all,
            *root_row,
            *panels,
            across_1,
            below_2a,
            below_2b,
            root_across,
            gated=3,
        )
        root_row = (root_inverse, root_beside, root_across_late, root_both)
        t_row = lax.all_gather(t, "col", axis=1, tiled=True)
        far = move(far_part, lambda r, c: (r ^ 1, c) if r >= 1 else None)
        below_3a = down(below_2a, 3)
        below_2 = jnp.concatenate((below_2a, below_2b), 0)
        across_2 = move(below_2, lambda r, c: (r, c ^ 2) if r == c and r in (0, 1) else None)
        across_3 = move(root_across_late, lambda r, c: (0, 2) if (r, c) == (3, 2) else None)

        near_part, own = local_call(
            cross_kernel,
            [ANY] * 4 + [VMEM],
            [t_block, shape((w, h), F32)],
            [pltpu.VMEM((2, h, h), BF16), dma((2,))],
            *root_row,
            t_t,
        )
        onward, below_2b = local_call(
            functools.partial(onward_kernel, deps=5),
            [ANY] * 4 + [VMEM, VMEM],
            [t_block],
            [pltpu.VMEM((h, h), BF16), dma],
            *root_row,
            t_t,
            far,
            near_part,
            across_2,
            across_3,
            below_3a,
            below_2b,
            gated=1,
        )
        last = move(onward, lambda r, c: (r - 2, c))
        near = move(near_part, lambda r, c: (r - 1, c) if r == 3 else None)
        below_3b = down(below_2b, 3)

        far_part, child_near_part, child_on, child_own = local_call(
            child_kernel,
            [VMEM] * 4,
            [child_block, child_block, shape((w, w), F32), shape((w, w), F32)],
            [pltpu.VMEM((w, w), BF16)],
            t_t,
            t_row,
            child_inverse,
            child_row,
            onward,
        )
        child_far = move(far_part, lambda r, c: (r ^ 1, c))
        (root_sum,) = local_call(
            diagonal_kernel,
            [],
            [shape((h, h), F32)],
            [pltpu.VMEM((h, h), BF16), pltpu.VMEM((h, h), BF16), dma((2,))],
            *root_row,
            far_part,
        )
        (child_onward,) = local_call(
            child_onward_kernel,
            [VMEM] * 2,
            [child_block],
            [],
            child_on,
            child_far,
            near,
            last,
            below_3b,
        )
        child_last = move(child_onward, lambda r, c: (r ^ 2, c))
        child_near = move(child_near_part, lambda r, c: (r ^ 1, c))

        below_3 = jnp.concatenate((below_3a, below_3b), 0)
        held = (below_1, below_2, below_3)
        across = (across_1, across_2, across_3)
        (picked,) = local_call(
            pick_kernel,
            [],
            [shape((3 * h, h), BF16)],
            [dma((3,))],
            *held,
            *across,
            child_onward,
            out_specs=[ANY],
        )
        beside = move(picked, lambda r, c: (r, c ^ 1) if r in (c, c ^ 2) and r < 3 else None)
        (sigma_cross,) = local_call(
            cross_end_kernel,
            [SMEM] + [VMEM] * 4,
            [shape((h, w), BF16)],
            [],
            structure,
            own,
            far,
            near,
            last,
        )
        (sigma_root,) = local_call(
            root_kernel,
            [VMEM],
            [shape((h, h), BF16)],
            [
                pltpu.VMEM((h, h), F32),
                pltpu.VMEM((3, h, h), BF16),
                pltpu.VMEM((3, h, h), BF16),
                dma((3,)),
                dma((3,)),
            ],
            root_sum,
            *held,
            *across,
            beside,
        )
        (sigma_child,) = local_call(
            child_end_kernel,
            [VMEM] * 3,
            [shape((w, w), F32)],
            [],
            child_own,
            child_near,
            child_last,
        )
        return (sigma_root, sigma_cross, sigma_child)

    return on_device


def solution(mesh):
    square = mesh.shape["row"] == N and mesh.shape["col"] == N
    spec = P(("fields", "row"), "col")
    return jax.shard_map(
        square_plan(mesh.shape["fields"]) if square else gather_plan,
        mesh=mesh,
        in_specs=(spec, spec, spec, P(("fields", "row"))),
        out_specs=(spec, spec, spec),
        check_vma=False,
    )
```

```python
import functools

import jax
import jax.numpy as jnp
from jax import lax
from jax.experimental import pallas as pl
from jax.experimental.pallas import tpu as pltpu
from jax.sharding import PartitionSpec as P

BLOCK = 128
AXES = ("fields", "row", "col")
BF16 = jnp.bfloat16
F32 = jnp.float32
TILE = 256
N = 4
VMEM_BYTES = 40 * 1024 * 1024


def inner_dot(left_part, right_part):
    return lax.dot_general(
        left_part, right_part, (((0,), (0,)), ((), ())), preferred_element_type=F32
    )


def dot(a, b):
    return jnp.dot(a, b, preferred_element_type=F32)


def mask_panel(panel, structure):
    kept_rows = jnp.repeat(structure, BLOCK)[:, None] > 0
    return kept_rows, jnp.where(kept_rows, panel, jnp.zeros_like(panel))


def gather_plan(root_inverse, child_inverse, panel, structure):
    kept_rows, panel_kept = mask_panel(panel, structure)
    root_full, child_rows, panel_full = (
        lax.all_gather(root_inverse, "col", axis=1, tiled=True),
        lax.all_gather(child_inverse, "col", axis=1, tiled=True),
        lax.all_gather(panel_kept, "col", axis=1, tiled=True),
    )
    root_sum = lax.psum_scatter(
        inner_dot(root_full, root_inverse), "row", scatter_dimension=0, tiled=True
    )
    sigma_root = root_sum.astype(BF16)
    sigma_rows = lax.all_gather(sigma_root, "col", axis=1, tiled=True)
    cross_sum = jnp.dot(
        sigma_rows,
        lax.all_gather(panel_kept, "row", axis=0, tiled=True),
        preferred_element_type=F32,
    )
    sigma_cross = jnp.where(kept_rows, -cross_sum, jnp.zeros_like(cross_sum)).astype(BF16)
    sigma_child = lax.psum_scatter(
        (inner_dot(child_rows, child_inverse) - inner_dot(panel_full, sigma_cross)).astype(BF16),
        "row",
        scatter_dimension=0,
        tiled=True,
    ).astype(F32)
    return (sigma_root, sigma_cross, sigma_child)


def position():
    return lax.axis_index("row"), lax.axis_index("col")


def start(src, dst, sem):
    pltpu.make_async_copy(src, dst, sem).start()


def wait(src, dst, sem):
    pltpu.make_async_copy(src, dst, sem).wait()


def start_picked(refs, index, dst, sem):
    for m, ref in enumerate(refs):

        @pl.when(index == m)
        def _():
            start(ref, dst, sem)


def tile(i):
    return pl.ds(pl.multiple_of(i * TILE, TILE), TILE)


def product_kernel(l0, l1, l2, l3, p0, p1, p2, p3, *refs, deps, gated):
    t_ref, tt_ref, sent_ref = refs[deps + gated : deps + gated + 3]
    rows, panels, acc, row_sems, panel_sems = refs[deps + 2 * gated + 3 :]
    r, c = position()
    for m, ref in enumerate((l0, l1, l2, l3)):
        j = c ^ m

        @pl.when(j <= r)
        def _():
            start(ref, rows.at[r - j], row_sems.at[r - j])

    for s, ref in enumerate((p0, p1, p2, p3)):

        @pl.when(s <= r)
        def _():
            start(ref, panels.at[s], panel_sems.at[s])

    for s in range(N):

        @pl.when(s <= r)
        def _():
            wait(l0, rows.at[s], row_sems.at[s])
            wait(p0, panels.at[s], panel_sems.at[s])

            @pl.loop(0, acc.shape[0] // TILE)
            def _(i):
                term = dot(rows[s, tile(i), :], panels[s])
                if s > 0:
                    term = term + acc[tile(i), :]
                acc[tile(i), :] = term

    @pl.loop(0, acc.shape[0] // TILE)
    def _(i):
        value = acc[tile(i), :]
        t_ref[tile(i), :] = value.astype(BF16)
        tt_ref[:, tile(i)] = value.T.astype(BF16)

    @pl.when(r == 3)
    def _():
        @pl.loop(0, tt_ref.shape[0] // TILE)
        def _(i):
            sent_ref[tile(i), :] = dot(tt_ref[tile(i), :], rows[3]).astype(BF16)


def own_kernel(l0, l1, l2, l3, tt_ref, own_ref, block, sem):
    r, c = position()
    start_picked((l0, l1, l2, l3), r ^ c, block, sem)
    wait(l0, block, sem)

    @pl.loop(0, tt_ref.shape[0] // TILE)
    def _(i):
        own_ref[tile(i), :] = dot(tt_ref[tile(i), :], block[...])


def chain_kernel(l0, l1, l2, l3, tt_ref, came_ref, *refs, step, deps, gated):
    sent_ref = refs[deps + gated]
    block, sem = refs[deps + 2 * gated + 1 :]
    r, c = position()
    i = step + r - 3

    @pl.when(i >= 0)
    def _():
        start_picked((l0, l1, l2, l3), i ^ c, block, sem)
        wait(l0, block, sem)

        @pl.when(r == 3)
        def _():
            @pl.loop(0, tt_ref.shape[0] // TILE)
            def _(j):
                sent_ref[tile(j), :] = dot(tt_ref[tile(j), :], block[...]).astype(BF16)

        @pl.when(r < 3)
        def _():
            @pl.loop(0, tt_ref.shape[0] // TILE)
            def _(j):
                term = dot(tt_ref[tile(j), :], block[...])
                sent_ref[tile(j), :] = (term + came_ref[tile(j), :].astype(F32)).astype(BF16)


def child_kernel(
    tt_ref, t_row_ref, child_ref, child_row_ref, _dep, far_ref, near_ref, onward_ref, own_ref, child_t
):
    r, _ = position()
    w = child_ref.shape[1]
    child_t[...] = child_ref[...].astype(F32).T.astype(BF16)
    for flip, ref in ((3, far_ref), (1, near_ref), (2, onward_ref), (0, own_ref)):
        columns = pl.ds(pl.multiple_of((r ^ flip) * w, w), w)

        @pl.loop(0, w // TILE)
        def _(i):
            term = dot(tt_ref[tile(i), :], t_row_ref[:, columns])
            term = term + dot(child_t[tile(i), :], child_row_ref[:, columns])
            ref[tile(i), :] = term.astype(ref.dtype)


def child_onward_kernel(own_ref, far_ref, _dep, out_ref):
    out_ref[...] = (own_ref[...] + far_ref[...].astype(F32)).astype(BF16)


def diagonal_kernel(l0, l1, l2, l3, _dep, acc_ref, left, held, sems):
    r, c = position()

    @pl.when(c <= r)
    def _():
        start_picked((l0, l1, l2, l3), r ^ c, left, sems.at[0])
        start(l0, held, sems.at[1])
        wait(l0, left, sems.at[0])
        wait(l0, held, sems.at[1])

        @pl.loop(0, acc_ref.shape[0] // TILE)
        def _(i):
            acc_ref[tile(i), :] = inner_dot(left[:, tile(i)], held[...])

    @pl.when(c > r)
    def _():
        acc_ref[...] = jnp.zeros_like(acc_ref)


def root_kernel(acc_ref, h1, h2, h3, x1, x2, x3, b1, b23, out_ref, acc, left, held, left_sems, held_sems):
    r, c = position()
    rows = h1.shape[0]
    refs = ((h1, x1, b1), (h2, x2, b23.at[:rows]), (h3, x3, b23.at[rows:]))
    needed = [(r + s < N) & (c <= r + s) for s in (1, 2, 3)]
    for s, places in enumerate(refs):

        @pl.when(needed[s])
        def _():
            start_picked(places, source(r, c), left.at[s], left_sems.at[s])
            start(places[0], held.at[s], held_sems.at[s])

    acc[...] = acc_ref[...]
    for s in range(3):

        @pl.when(needed[s])
        def _():
            wait(h1, left.at[s], left_sems.at[s])
            wait(h1, held.at[s], held_sems.at[s])

            @pl.loop(0, acc.shape[0] // TILE)
            def _(i):
                acc[tile(i), :] += inner_dot(left[s, :, tile(i)], held[s])

    out_ref[...] = acc[...].astype(BF16)


def source(r, c):
    return jnp.where(c == r, 0, jnp.where(c == (r ^ 2), 1, 2))


def cross_end_kernel(structure, own_ref, came_ref, out_ref):
    for b in range(own_ref.shape[1] // BLOCK):
        rows = slice(b * BLOCK, (b + 1) * BLOCK)
        total = own_ref[:, rows] + came_ref[:, rows].astype(F32)
        kept = structure[b] > 0
        out_ref[rows, :] = jnp.where(kept, -total.T, jnp.zeros_like(total.T)).astype(BF16)


def child_end_kernel(own_ref, near_ref, last_ref, out_ref):
    total = own_ref[...] + near_ref[...].astype(F32) + last_ref[...].astype(F32)
    out_ref[...] = total.T


ANY = pl.BlockSpec(memory_space=pl.ANY)
VMEM = pl.BlockSpec(memory_space=pltpu.VMEM)
SMEM = pl.BlockSpec(memory_space=pltpu.SMEM)


def local_call(kernel, in_specs, outs, scratch, *args, gated=0, out_specs=None):
    first = len(args) - gated
    outs = outs + [jax.ShapeDtypeStruct(x.shape, x.dtype) for x in args[first:]]
    return pl.pallas_call(
        kernel,
        out_shape=outs,
        in_specs=in_specs + [ANY] * (len(args) - len(in_specs)),
        out_specs=(out_specs or [VMEM] * (len(outs) - gated)) + [ANY] * gated,
        scratch_shapes=scratch,
        input_output_aliases={first + i: len(outs) - gated + i for i in range(gated)},
        compiler_params=pltpu.CompilerParams(vmem_limit_bytes=VMEM_BYTES),
        cost_estimate=pl.CostEstimate(flops=1, bytes_accessed=1, transcendentals=0),
    )(*args)


def together(*arrays, earlier=()):
    k = len(arrays)
    return pl.pallas_call(
        lambda *refs: None,
        out_shape=[jax.ShapeDtypeStruct(x.shape, x.dtype) for x in arrays],
        in_specs=[ANY] * (k + len(earlier)),
        out_specs=[ANY] * k,
        input_output_aliases={i: i for i in range(k)},
    )(*arrays, *earlier)


def square_plan(fields):
    n = N

    def move(x, target):
        pairs = []
        for f in range(fields):
            for r in range(n):
                for c in range(n):
                    to = target(r, c)
                    if to is not None and 0 <= to[0] < n:
                        pairs.append(((f * n + r) * n + c, (f * n + to[0]) * n + to[1]))
        return lax.ppermute(x, AXES, pairs)

    def up(x, s):
        return move(x, lambda r, c: (r + 1, c) if r >= s - 1 else None)

    def down(x, s):
        def target(r, c):
            k = r + s - 1
            return (r - 1, c) if k < n and c <= k else None

        return move(x, target)

    def on_device(root_inverse, child_inverse, panel, structure):
        h, w = panel.shape
        half = h // 2
        lower = lambda r, c: c <= r
        shape = jax.ShapeDtypeStruct
        dma = pltpu.SemaphoreType.DMA
        t_block, child_block = shape((w, h), BF16), shape((w, w), BF16)

        _, panel_kept = mask_panel(panel, structure)
        child_row = lax.all_gather(child_inverse, "col", axis=1, tiled=True)
        panel_1 = up(panel_kept, 1)
        root_across = move(root_inverse, lambda r, c: (r, c ^ 2) if lower(r, c) else None)
        below_1 = down(root_inverse, 1)
        root_beside = move(root_inverse, lambda r, c: (r, c ^ 1) if lower(r, c) else None)
        panel_2 = up(panel_1, 2)
        (panel_2,) = together(panel_2, earlier=(below_1, root_across, root_beside))
        panel_3 = up(panel_2, 3)
        root_both = move(root_across, lambda r, c: (r, c ^ 1) if lower(r, c ^ 2) else None)
        below_2a = down(below_1[:half], 2)
        across_1 = move(below_1, lambda r, c: (r, c ^ 2) if r == c and r in (1, 2) else None)
        across_3 = move(root_across, lambda r, c: (0, 2) if (r, c) == (3, 2) else None)

        root_row = (root_inverse, root_beside, root_across, root_both)
        panels = (panel_kept, panel_1, panel_2, panel_3)
        t, t_t, sent, below_1, below_2a = local_call(
            functools.partial(product_kernel, deps=1, gated=2),
            [ANY] * 8,
            [shape((h, w), BF16), t_block, t_block],
            [
                pltpu.VMEM((n, h, h), BF16),
                pltpu.VMEM((n, h, w), BF16),
                pltpu.VMEM((h, w), F32),
                dma((n,)),
                dma((n,)),
            ],
            *root_row,
            *panels,
            across_1,
            below_1,
            below_2a,
            gated=2,
        )
        t_row = lax.all_gather(t, "col", axis=1, tiled=True)
        step = lambda x, q: move(x, lambda r, c: (r - 1, c) if q + r - 3 >= 0 else None)
        chain = [ANY] * 4 + [VMEM] * 2
        came = step(sent, 0)
        below_2b = down(below_1[half:], 2)
        below_3a = down(below_2a, 3)
        (own,) = local_call(
            own_kernel,
            [ANY] * 4 + [VMEM],
            [shape((w, h), F32)],
            [pltpu.VMEM((h, h), BF16), dma],
            *root_row,
            t_t,
        )
        sent, below_2b, across_1 = local_call(
            functools.partial(chain_kernel, step=1, deps=3, gated=2),
            chain,
            [t_block],
            [pltpu.VMEM((h, h), BF16), dma],
            *root_row,
            t_t,
            came,
            own,
            below_3a,
            across_3,
            below_2b,
            across_1,
            gated=2,
        )
        came = step(sent, 1)
        below_3b = down(below_2b, 3)
        below_2 = jnp.concatenate((below_2a, below_2b), 0)
        across_2 = move(below_2, lambda r, c: (r, c ^ 2) if r == c and r in (0, 1) else None)
        c_is_r = lax.axis_index("col") == lax.axis_index("row")

        def to_beside(held, across, last_row):
            return move(
                jnp.where(c_is_r, held, across),
                lambda r, c: (r, c ^ 1) if r in (c, c ^ 2) and r <= last_row else None,
            )

        beside_1 = to_beside(below_1, across_1, 2)

        far_part, near_part, child_on, child_own = local_call(
            child_kernel,
            [VMEM] * 4,
            [child_block, child_block, shape((w, w), F32), shape((w, w), F32)],
            [pltpu.VMEM((w, w), BF16)],
            t_t,
            t_row,
            child_inverse,
            child_row,
            sent,
        )
        child_far = move(far_part, lambda r, c: (r ^ 1, c))
        (root_sum,) = local_call(
            diagonal_kernel,
            [],
            [shape((h, h), F32)],
            [pltpu.VMEM((h, h), BF16), pltpu.VMEM((h, h), BF16), dma((2,))],
            *root_row,
            far_part,
        )
        sent, across_2 = local_call(
            functools.partial(chain_kernel, step=2, deps=3, gated=1),
            chain,
            [t_block],
            [pltpu.VMEM((h, h), BF16), dma],
            *root_row,
            t_t,
            came,
            below_3b,
            child_far,
            beside_1,
            across_2,
            gated=1,
        )
        came = step(sent, 2)
        (child_onward,) = local_call(
            child_onward_kernel, [VMEM] * 2, [child_block], [], child_on, child_far, sent
        )
        child_last = move(child_onward, lambda r, c: (r ^ 2, c))
        child_near = move(near_part, lambda r, c: (r ^ 1, c))
        below_3 = jnp.concatenate((below_3a, below_3b), 0)
        beside_23 = to_beside(
            jnp.concatenate((below_2, below_3), 0), jnp.concatenate((across_2, across_3), 0), 1
        )
        (sigma_cross,) = local_call(
            cross_end_kernel,
            [SMEM] + [VMEM] * 2,
            [shape((h, w), BF16)],
            [],
            structure,
            own,
            came,
        )
        (sigma_root,) = local_call(
            root_kernel,
            [VMEM],
            [shape((h, h), BF16)],
            [
                pltpu.VMEM((h, h), F32),
                pltpu.VMEM((3, h, h), BF16),
                pltpu.VMEM((3, h, h), BF16),
                dma((3,)),
                dma((3,)),
            ],
            root_sum,
            below_1,
            below_2,
            below_3,
            across_1,
            across_2,
            across_3,
            beside_1,
            beside_23,
        )
        (sigma_child,) = local_call(
            child_end_kernel,
            [VMEM] * 3,
            [shape((w, w), F32)],
            [],
            child_own,
            child_near,
            child_last,
        )
        return (sigma_root, sigma_cross, sigma_child)

    return on_device


def solution(mesh):
    square = mesh.shape["row"] == N and mesh.shape["col"] == N
    spec = P(("fields", "row"), "col")
    return jax.shard_map(
        square_plan(mesh.shape["fields"]) if square else gather_plan,
        mesh=mesh,
        in_specs=(spec, spec, spec, P(("fields", "row"))),
        out_specs=(spec, spec, spec),
        check_vma=False,
    )
```

```python
import functools

import jax
import jax.numpy as jnp
from jax import lax
from jax.experimental import pallas as pl
from jax.experimental.pallas import tpu as pltpu
from jax.sharding import PartitionSpec as P

BLOCK = 128
AXES = ("fields", "row", "col")
BF16 = jnp.bfloat16
F32 = jnp.float32
TILE = 256
N = 4
VMEM_BYTES = 40 * 1024 * 1024


def inner_dot(left_part, right_part):
    return lax.dot_general(
        left_part, right_part, (((0,), (0,)), ((), ())), preferred_element_type=F32
    )


def dot(a, b):
    return jnp.dot(a, b, preferred_element_type=F32)


def mask_panel(panel, structure):
    kept_rows = jnp.repeat(structure, BLOCK)[:, None] > 0
    return kept_rows, jnp.where(kept_rows, panel, jnp.zeros_like(panel))


def gather_plan(root_inverse, child_inverse, panel, structure):
    kept_rows, panel_kept = mask_panel(panel, structure)
    root_full, child_rows, panel_full = (
        lax.all_gather(root_inverse, "col", axis=1, tiled=True),
        lax.all_gather(child_inverse, "col", axis=1, tiled=True),
        lax.all_gather(panel_kept, "col", axis=1, tiled=True),
    )
    root_sum = lax.psum_scatter(
        inner_dot(root_full, root_inverse), "row", scatter_dimension=0, tiled=True
    )
    sigma_root = root_sum.astype(BF16)
    sigma_rows = lax.all_gather(sigma_root, "col", axis=1, tiled=True)
    cross_sum = jnp.dot(
        sigma_rows,
        lax.all_gather(panel_kept, "row", axis=0, tiled=True),
        preferred_element_type=F32,
    )
    sigma_cross = jnp.where(kept_rows, -cross_sum, jnp.zeros_like(cross_sum)).astype(BF16)
    sigma_child = lax.psum_scatter(
        (inner_dot(child_rows, child_inverse) - inner_dot(panel_full, sigma_cross)).astype(BF16),
        "row",
        scatter_dimension=0,
        tiled=True,
    ).astype(F32)
    return (sigma_root, sigma_cross, sigma_child)


def position():
    return lax.axis_index("row"), lax.axis_index("col")


def start(src, dst, sem):
    pltpu.make_async_copy(src, dst, sem).start()


def wait(src, dst, sem):
    pltpu.make_async_copy(src, dst, sem).wait()


def start_picked(refs, index, dst, sem):
    for m, ref in enumerate(refs):

        @pl.when(index == m)
        def _():
            start(ref, dst, sem)


def tile(i):
    return pl.ds(pl.multiple_of(i * TILE, TILE), TILE)


def product_kernel(l0, l1, l2, l3, p0, p1, p2, p3, *refs, deps, gated):
    below = refs[deps]
    t_ref, tt_ref, sent_ref = refs[deps + gated : deps + gated + 3]
    rows, panels, acc, row_sems, panel_sems, sem = refs[deps + 2 * gated + 3 :]
    r, c = position()
    half = below.at[sent_ref.shape[0] :]

    @pl.when((r == 1) | (r == 2))
    def _():
        start(half, sent_ref, sem)

    for m, ref in enumerate((l0, l1, l2, l3)):
        j = c ^ m

        @pl.when(j <= r)
        def _():
            start(ref, rows.at[r - j], row_sems.at[r - j])

    for s, ref in enumerate((p0, p1, p2, p3)):

        @pl.when(s <= r)
        def _():
            start(ref, panels.at[s], panel_sems.at[s])

    for s in range(N):

        @pl.when(s <= r)
        def _():
            wait(l0, rows.at[s], row_sems.at[s])
            wait(p0, panels.at[s], panel_sems.at[s])

            @pl.loop(0, acc.shape[0] // TILE)
            def _(i):
                term = dot(rows[s, tile(i), :], panels[s])
                if s > 0:
                    term = term + acc[tile(i), :]
                acc[tile(i), :] = term

    @pl.loop(0, acc.shape[0] // TILE)
    def _(i):
        value = acc[tile(i), :]
        t_ref[tile(i), :] = value.astype(BF16)
        tt_ref[:, tile(i)] = value.T.astype(BF16)

    @pl.when(r == 3)
    def _():
        @pl.loop(0, tt_ref.shape[0] // TILE)
        def _(i):
            sent_ref[tile(i), :] = dot(tt_ref[tile(i), :], rows[3]).astype(BF16)

    @pl.when((r == 1) | (r == 2))
    def _():
        wait(half, sent_ref, sem)


def own_kernel(l0, l1, l2, l3, tt_ref, own_ref, block, sem):
    r, c = position()
    start_picked((l0, l1, l2, l3), r ^ c, block, sem)
    wait(l0, block, sem)

    @pl.loop(0, tt_ref.shape[0] // TILE)
    def _(i):
        own_ref[tile(i), :] = dot(tt_ref[tile(i), :], block[...])


def chain_kernel(l0, l1, l2, l3, tt_ref, came_ref, *refs, step, deps, gated):
    sent_ref = refs[deps + gated]
    block, sem = refs[deps + 2 * gated + 1 :]
    r, c = position()
    i = step + r - 3

    @pl.when(i >= 0)
    def _():
        start_picked((l0, l1, l2, l3), i ^ c, block, sem)
        wait(l0, block, sem)

        @pl.when(r == 3)
        def _():
            @pl.loop(0, tt_ref.shape[0] // TILE)
            def _(j):
                sent_ref[tile(j), :] = dot(tt_ref[tile(j), :], block[...]).astype(BF16)

        @pl.when(r < 3)
        def _():
            @pl.loop(0, tt_ref.shape[0] // TILE)
            def _(j):
                term = dot(tt_ref[tile(j), :], block[...])
                sent_ref[tile(j), :] = (term + came_ref[tile(j), :].astype(F32)).astype(BF16)

    @pl.when((i < 0) & (r == 1))
    def _():
        sent_ref[...] = came_ref[...]


def child_kernel(
    tt_ref, t_row_ref, child_ref, child_row_ref, _dep, far_ref, near_ref, onward_ref, own_ref, child_t
):
    r, _ = position()
    w = child_ref.shape[1]
    child_t[...] = child_ref[...].astype(F32).T.astype(BF16)
    for flip, ref in ((3, far_ref), (1, near_ref), (2, onward_ref), (0, own_ref)):
        columns = pl.ds(pl.multiple_of((r ^ flip) * w, w), w)

        @pl.loop(0, w // TILE)
        def _(i):
            term = dot(tt_ref[tile(i), :], t_row_ref[:, columns])
            term = term + dot(child_t[tile(i), :], child_row_ref[:, columns])
            ref[tile(i), :] = term.astype(ref.dtype)


def child_onward_kernel(own_ref, far_ref, _dep, out_ref):
    out_ref[...] = (own_ref[...] + far_ref[...].astype(F32)).astype(BF16)


def diagonal_kernel(l0, l1, l2, l3, _dep, acc_ref, left, held, sems):
    r, c = position()

    @pl.when(c <= r)
    def _():
        start_picked((l0, l1, l2, l3), r ^ c, left, sems.at[0])
        start(l0, held, sems.at[1])
        wait(l0, left, sems.at[0])
        wait(l0, held, sems.at[1])

        @pl.loop(0, acc_ref.shape[0] // TILE)
        def _(i):
            acc_ref[tile(i), :] = inner_dot(left[:, tile(i)], held[...])

    @pl.when(c > r)
    def _():
        acc_ref[...] = jnp.zeros_like(acc_ref)


def root_kernel(acc_ref, h1, h2, h3, b1, b2, b3, x1, x2, x3, f1, f2, f3, out_ref, acc, left, held, left_sems, held_sems):
    r, c = position()
    refs = ((h1, b1, x1, f1), (h2, b2, x2, f2), (h3, b3, x3, f3))
    needed = [(r + s < N) & (c <= r + s) for s in (1, 2, 3)]
    for s, places in enumerate(refs):

        @pl.when(needed[s])
        def _():
            start_picked(places, r ^ c, left.at[s], left_sems.at[s])
            start(places[0], held.at[s], held_sems.at[s])

    acc[...] = acc_ref[...]
    for s in range(3):

        @pl.when(needed[s])
        def _():
            wait(h1, left.at[s], left_sems.at[s])
            wait(h1, held.at[s], held_sems.at[s])

            @pl.loop(0, acc.shape[0] // TILE)
            def _(i):
                acc[tile(i), :] += inner_dot(left[s, :, tile(i)], held[s])

    out_ref[...] = acc[...].astype(BF16)


def cross_end_kernel(structure, own_ref, came_ref, out_ref):
    for b in range(own_ref.shape[1] // BLOCK):
        rows = slice(b * BLOCK, (b + 1) * BLOCK)
        total = own_ref[:, rows] + came_ref[:, rows].astype(F32)
        kept = structure[b] > 0
        out_ref[rows, :] = jnp.where(kept, -total.T, jnp.zeros_like(total.T)).astype(BF16)


def child_end_kernel(own_ref, near_ref, last_ref, _dep, out_ref):
    total = own_ref[...] + near_ref[...].astype(F32) + last_ref[...].astype(F32)
    out_ref[...] = total.T


ANY = pl.BlockSpec(memory_space=pl.ANY)
VMEM = pl.BlockSpec(memory_space=pltpu.VMEM)
SMEM = pl.BlockSpec(memory_space=pltpu.SMEM)


def local_call(kernel, in_specs, outs, scratch, *args, gated=0, out_specs=None):
    first = len(args) - gated
    outs = outs + [jax.ShapeDtypeStruct(x.shape, x.dtype) for x in args[first:]]
    return pl.pallas_call(
        kernel,
        out_shape=outs,
        in_specs=in_specs + [ANY] * (len(args) - len(in_specs)),
        out_specs=(out_specs or [VMEM] * (len(outs) - gated)) + [ANY] * gated,
        scratch_shapes=scratch,
        input_output_aliases={first + i: len(outs) - gated + i for i in range(gated)},
        compiler_params=pltpu.CompilerParams(vmem_limit_bytes=VMEM_BYTES),
        cost_estimate=pl.CostEstimate(flops=1, bytes_accessed=1, transcendentals=0),
    )(*args)


def together(*arrays, earlier=()):
    k = len(arrays)
    return pl.pallas_call(
        lambda *refs: None,
        out_shape=[jax.ShapeDtypeStruct(x.shape, x.dtype) for x in arrays],
        in_specs=[ANY] * (k + len(earlier)),
        out_specs=[ANY] * k,
        input_output_aliases={i: i for i in range(k)},
    )(*arrays, *earlier)


def square_plan(fields):
    n = N

    def move(x, target):
        pairs = []
        for f in range(fields):
            for r in range(n):
                for c in range(n):
                    to = target(r, c)
                    if to is not None and 0 <= to[0] < n:
                        pairs.append(((f * n + r) * n + c, (f * n + to[0]) * n + to[1]))
        return lax.ppermute(x, AXES, pairs)

    def up(x, s):
        return move(x, lambda r, c: (r + 1, c) if r >= s - 1 else None)

    def down(x, s):
        def target(r, c):
            k = r + s - 1
            return (r - 1, c) if k < n and c <= k else None

        return move(x, target)

    def on_device(root_inverse, child_inverse, panel, structure):
        h, w = panel.shape
        half = h // 2
        lower = lambda r, c: c <= r
        shape = jax.ShapeDtypeStruct
        dma = pltpu.SemaphoreType.DMA
        t_block, child_block = shape((w, h), BF16), shape((w, w), BF16)

        _, panel_kept = mask_panel(panel, structure)
        child_row = lax.all_gather(child_inverse, "col", axis=1, tiled=True)
        panel_1 = up(panel_kept, 1)
        root_across = move(root_inverse, lambda r, c: (r, c ^ 2) if lower(r, c) else None)
        below_1 = down(root_inverse, 1)
        (root_late,) = together(root_inverse, earlier=(panel_1,))
        root_beside = move(root_late, lambda r, c: (r, c ^ 1) if lower(r, c) else None)
        across_3 = move(root_late, lambda r, c: (0, 2) if (r, c) == (3, 0) else None)
        panel_2 = up(panel_1, 2)
        (panel_2,) = together(panel_2, earlier=(below_1, root_across, root_beside))
        panel_3 = up(panel_2, 3)
        root_both = move(root_across, lambda r, c: (r, c ^ 1) if lower(r, c ^ 2) else None)
        below_2a = down(below_1[:half], 2)

        def to_across(x, rows):
            return move(x, lambda r, c: (r, c ^ 2) if r == c and r in rows else None)

        def to_beside(x, rows):
            return move(x, lambda r, c: (r, c ^ 1) if r == c and r in rows else None)

        def on_beside(x, rows):
            return move(x, lambda r, c: (r, c ^ 1) if r == c ^ 2 and r in rows else None)

        across_1 = to_across(below_1, (1, 2))
        beside_1 = to_beside(below_1, (0, 1, 2))

        root_row = (root_inverse, root_beside, root_across, root_both)
        panels = (panel_kept, panel_1, panel_2, panel_3)
        t, t_t, sent, below_1, below_2a = local_call(
            functools.partial(product_kernel, deps=2, gated=2),
            [ANY] * 8,
            [shape((h, w), BF16), t_block, t_block],
            [
                pltpu.VMEM((n, h, h), BF16),
                pltpu.VMEM((n, h, w), BF16),
                pltpu.VMEM((h, w), F32),
                dma((n,)),
                dma((n,)),
                dma,
            ],
            *root_row,
            *panels,
            across_1,
            beside_1,
            below_1,
            below_2a,
            gated=2,
        )
        t_row = lax.all_gather(t, "col", axis=1, tiled=True)
        step = lambda x: move(x, lambda r, c: (r - 1, c))
        chain = [ANY] * 4 + [VMEM] * 2
        below_2b = came = step(sent)
        below_3a = down(below_2a, 3)
        far_1 = on_beside(across_1, (1, 2))
        (own,) = local_call(
            own_kernel,
            [ANY] * 4 + [VMEM],
            [shape((w, h), F32)],
            [pltpu.VMEM((h, h), BF16), dma],
            *root_row,
            t_t,
        )
        sent, below_2a = local_call(
            functools.partial(chain_kernel, step=1, deps=4, gated=1),
            chain,
            [t_block],
            [pltpu.VMEM((h, h), BF16), dma],
            *root_row,
            t_t,
            came,
            own,
            below_3a,
            far_1,
            across_3,
            below_2a,
            gated=1,
        )
        below_2 = jnp.concatenate((below_2a, below_2b), 0)
        below_3b = came = step(sent)
        across_2 = to_across(below_2, (0, 1))
        beside_2 = to_beside(below_2, (0, 1))

        far_part, near_part, child_on, child_own = local_call(
            child_kernel,
            [VMEM] * 4,
            [child_block, child_block, shape((w, w), F32), shape((w, w), F32)],
            [pltpu.VMEM((w, w), BF16)],
            t_t,
            t_row,
            child_inverse,
            child_row,
            sent,
        )
        child_far = move(far_part, lambda r, c: (r ^ 1, c))
        child_near = move(near_part, lambda r, c: (r ^ 1, c))
        (root_sum,) = local_call(
            diagonal_kernel,
            [],
            [shape((h, h), F32)],
            [pltpu.VMEM((h, h), BF16), pltpu.VMEM((h, h), BF16), dma((2,))],
            *root_row,
            far_part,
        )
        sent, across_2, across_3, below_3a = local_call(
            functools.partial(chain_kernel, step=2, deps=3, gated=3),
            chain,
            [t_block],
            [pltpu.VMEM((h, h), BF16), dma],
            *root_row,
            t_t,
            came,
            child_far,
            child_near,
            beside_2,
            across_2,
            across_3,
            below_3a,
            gated=3,
        )
        came = step(sent)
        (child_onward,) = local_call(
            child_onward_kernel, [VMEM] * 2, [child_block], [], child_on, child_far, sent
        )
        child_last = move(child_onward, lambda r, c: (r ^ 2, c))
        below_3 = jnp.concatenate((below_3a, below_3b), 0)
        beside_3 = to_beside(below_3, (0,))
        far_2 = on_beside(across_2, (0, 1))
        far_3 = on_beside(across_3, (0,))
        (sigma_cross,) = local_call(
            cross_end_kernel,
            [SMEM] + [VMEM] * 2,
            [shape((h, w), BF16)],
            [],
            structure,
            own,
            came,
        )
        (sigma_root,) = local_call(
            root_kernel,
            [VMEM],
            [shape((h, h), BF16)],
            [
                pltpu.VMEM((h, h), F32),
                pltpu.VMEM((3, h, h), BF16),
                pltpu.VMEM((3, h, h), BF16),
                dma((3,)),
                dma((3,)),
            ],
            root_sum,
            below_1,
            below_2,
            below_3,
            beside_1,
            beside_2,
            beside_3,
            across_1,
            across_2,
            across_3,
            far_1,
            far_2,
            far_3,
        )
        (sigma_child,) = local_call(
            child_end_kernel,
            [VMEM] * 3,
            [shape((w, w), F32)],
            [],
            child_own,
            child_near,
            child_last,
            sigma_root,
        )
        return (sigma_root, sigma_cross, sigma_child)

    return on_device


def solution(mesh):
    square = mesh.shape["row"] == N and mesh.shape["col"] == N
    spec = P(("fields", "row"), "col")
    return jax.shard_map(
        square_plan(mesh.shape["fields"]) if square else gather_plan,
        mesh=mesh,
        in_specs=(spec, spec, spec, P(("fields", "row"))),
        out_specs=(spec, spec, spec),
        check_vma=False,
    )
```

```python
import functools

import jax
import jax.numpy as jnp
from jax import lax
from jax.experimental import pallas as pl
from jax.experimental.pallas import tpu as pltpu
from jax.sharding import PartitionSpec as P

BLOCK = 128
AXES = ("fields", "row", "col")
BF16 = jnp.bfloat16
F32 = jnp.float32
TILE = 256
N = 4
VMEM_BYTES = 40 * 1024 * 1024


def inner_dot(left_part, right_part):
    return lax.dot_general(
        left_part, right_part, (((0,), (0,)), ((), ())), preferred_element_type=F32
    )


def dot(a, b):
    return jnp.dot(a, b, preferred_element_type=F32)


def mask_panel(panel, structure):
    kept_rows = jnp.repeat(structure, BLOCK)[:, None] > 0
    return kept_rows, jnp.where(kept_rows, panel, jnp.zeros_like(panel))


def gather_plan(root_inverse, child_inverse, panel, structure):
    kept_rows, panel_kept = mask_panel(panel, structure)
    root_full, child_rows, panel_full = (
        lax.all_gather(root_inverse, "col", axis=1, tiled=True),
        lax.all_gather(child_inverse, "col", axis=1, tiled=True),
        lax.all_gather(panel_kept, "col", axis=1, tiled=True),
    )
    root_sum = lax.psum_scatter(
        inner_dot(root_full, root_inverse), "row", scatter_dimension=0, tiled=True
    )
    sigma_root = root_sum.astype(BF16)
    sigma_rows = lax.all_gather(sigma_root, "col", axis=1, tiled=True)
    cross_sum = jnp.dot(
        sigma_rows,
        lax.all_gather(panel_kept, "row", axis=0, tiled=True),
        preferred_element_type=F32,
    )
    sigma_cross = jnp.where(kept_rows, -cross_sum, jnp.zeros_like(cross_sum)).astype(BF16)
    sigma_child = lax.psum_scatter(
        (inner_dot(child_rows, child_inverse) - inner_dot(panel_full, sigma_cross)).astype(BF16),
        "row",
        scatter_dimension=0,
        tiled=True,
    ).astype(F32)
    return (sigma_root, sigma_cross, sigma_child)


def position():
    return lax.axis_index("row"), lax.axis_index("col")


def start(src, dst, sem):
    pltpu.make_async_copy(src, dst, sem).start()


def wait(src, dst, sem):
    pltpu.make_async_copy(src, dst, sem).wait()


def start_picked(refs, index, dst, sem):
    for m, ref in enumerate(refs):

        @pl.when(index == m)
        def _():
            start(ref, dst, sem)


def tile(i):
    return pl.ds(pl.multiple_of(i * TILE, TILE), TILE)


def product_kernel(l0, l1, l2, l3, p0, p1, p2, p3, *refs, deps, gated):
    below = refs[deps]
    t_ref, tt_ref, sent_ref = refs[deps + gated : deps + gated + 3]
    rows, panels, acc, row_sems, panel_sems, sem = refs[deps + 2 * gated + 3 :]
    r, c = position()
    half = below.at[sent_ref.shape[0] :]

    @pl.when((r == 1) | (r == 2))
    def _():
        start(half, sent_ref, sem)

    for m, ref in enumerate((l0, l1, l2, l3)):
        j = c ^ m

        @pl.when(j <= r)
        def _():
            start(ref, rows.at[r - j], row_sems.at[r - j])

    for s, ref in enumerate((p0, p1, p2, p3)):

        @pl.when(s <= r)
        def _():
            start(ref, panels.at[s], panel_sems.at[s])

    for s in range(N):

        @pl.when(s <= r)
        def _():
            wait(l0, rows.at[s], row_sems.at[s])
            wait(p0, panels.at[s], panel_sems.at[s])

            @pl.loop(0, acc.shape[0] // TILE)
            def _(i):
                term = dot(rows[s, tile(i), :], panels[s])
                if s > 0:
                    term = term + acc[tile(i), :]
                acc[tile(i), :] = term

    @pl.loop(0, acc.shape[0] // TILE)
    def _(i):
        value = acc[tile(i), :]
        t_ref[tile(i), :] = value.astype(BF16)
        tt_ref[:, tile(i)] = value.T.astype(BF16)

    @pl.when(r == 3)
    def _():
        @pl.loop(0, tt_ref.shape[0] // TILE)
        def _(i):
            sent_ref[tile(i), :] = dot(tt_ref[tile(i), :], rows[3]).astype(BF16)

    @pl.when((r == 1) | (r == 2))
    def _():
        wait(half, sent_ref, sem)


def own_kernel(l0, l1, l2, l3, tt_ref, _in, own_ref, _out, block, sem):
    r, c = position()
    start_picked((l0, l1, l2, l3), r ^ c, block, sem)
    wait(l0, block, sem)

    @pl.loop(0, tt_ref.shape[0] // TILE)
    def _(i):
        own_ref[tile(i), :] = dot(tt_ref[tile(i), :], block[...])


def chain_kernel(l0, l1, l2, l3, tt_ref, came_ref, *refs, step, deps, gated):
    sent_ref = refs[deps + gated]
    block, sem = refs[deps + 2 * gated + 1 :]
    r, c = position()
    i = step + r - 3

    @pl.when(i >= 0)
    def _():
        start_picked((l0, l1, l2, l3), i ^ c, block, sem)
        wait(l0, block, sem)

        @pl.when(r == 3)
        def _():
            @pl.loop(0, tt_ref.shape[0] // TILE)
            def _(j):
                sent_ref[tile(j), :] = dot(tt_ref[tile(j), :], block[...]).astype(BF16)

        @pl.when(r < 3)
        def _():
            @pl.loop(0, tt_ref.shape[0] // TILE)
            def _(j):
                term = dot(tt_ref[tile(j), :], block[...])
                sent_ref[tile(j), :] = (term + came_ref[tile(j), :].astype(F32)).astype(BF16)

    @pl.when((i < 0) & (r == 1))
    def _():
        sent_ref[...] = came_ref[...]


def child_kernel(
    tt_ref, t_row_ref, child_ref, child_row_ref, _dep, far_ref, near_ref, onward_ref, own_ref, child_t
):
    r, _ = position()
    w = child_ref.shape[1]
    child_t[...] = child_ref[...].astype(F32).T.astype(BF16)
    for flip, ref in ((3, far_ref), (1, near_ref), (2, onward_ref), (0, own_ref)):
        columns = pl.ds(pl.multiple_of((r ^ flip) * w, w), w)

        @pl.loop(0, w // TILE)
        def _(i):
            term = dot(tt_ref[tile(i), :], t_row_ref[:, columns])
            term = term + dot(child_t[tile(i), :], child_row_ref[:, columns])
            ref[tile(i), :] = term.astype(ref.dtype)


def child_onward_kernel(own_ref, far_ref, _dep, out_ref):
    out_ref[...] = (own_ref[...] + far_ref[...].astype(F32)).astype(BF16)


def diagonal_kernel(l0, l1, l2, l3, _dep, acc_ref, left, held, sems):
    r, c = position()

    @pl.when(c <= r)
    def _():
        start_picked((l0, l1, l2, l3), r ^ c, left, sems.at[0])
        start(l0, held, sems.at[1])
        wait(l0, left, sems.at[0])
        wait(l0, held, sems.at[1])

        @pl.loop(0, acc_ref.shape[0] // TILE)
        def _(i):
            acc_ref[tile(i), :] = inner_dot(left[:, tile(i)], held[...])

    @pl.when(c > r)
    def _():
        acc_ref[...] = jnp.zeros_like(acc_ref)


def root_kernel(acc_ref, h1, h2, h3, b1, b2, b3, x1, x2, x3, f1, f2, f3, out_ref, acc, left, held, left_sems, held_sems):
    r, c = position()
    refs = ((h1, b1, x1, f1), (h2, b2, x2, f2), (h3, b3, x3, f3))
    needed = [(r + s < N) & (c <= r + s) for s in (1, 2, 3)]
    for s, places in enumerate(refs):

        @pl.when(needed[s])
        def _():
            start_picked(places, r ^ c, left.at[s], left_sems.at[s])
            start(places[0], held.at[s], held_sems.at[s])

    acc[...] = acc_ref[...]
    for s in range(3):

        @pl.when(needed[s])
        def _():
            wait(h1, left.at[s], left_sems.at[s])
            wait(h1, held.at[s], held_sems.at[s])

            @pl.loop(0, acc.shape[0] // TILE)
            def _(i):
                acc[tile(i), :] += inner_dot(left[s, :, tile(i)], held[s])

    out_ref[...] = acc[...].astype(BF16)


def cross_end_kernel(structure, own_ref, came_ref, out_ref):
    for b in range(own_ref.shape[1] // BLOCK):
        rows = slice(b * BLOCK, (b + 1) * BLOCK)
        total = own_ref[:, rows] + came_ref[:, rows].astype(F32)
        kept = structure[b] > 0
        out_ref[rows, :] = jnp.where(kept, -total.T, jnp.zeros_like(total.T)).astype(BF16)


def child_end_kernel(own_ref, near_ref, last_ref, _dep, out_ref):
    total = own_ref[...] + near_ref[...].astype(F32) + last_ref[...].astype(F32)
    out_ref[...] = total.T


ANY = pl.BlockSpec(memory_space=pl.ANY)
VMEM = pl.BlockSpec(memory_space=pltpu.VMEM)
SMEM = pl.BlockSpec(memory_space=pltpu.SMEM)


def local_call(kernel, in_specs, outs, scratch, *args, gated=0, out_specs=None):
    first = len(args) - gated
    outs = outs + [jax.ShapeDtypeStruct(x.shape, x.dtype) for x in args[first:]]
    return pl.pallas_call(
        kernel,
        out_shape=outs,
        in_specs=in_specs + [ANY] * (len(args) - len(in_specs)),
        out_specs=(out_specs or [VMEM] * (len(outs) - gated)) + [ANY] * gated,
        scratch_shapes=scratch,
        input_output_aliases={first + i: len(outs) - gated + i for i in range(gated)},
        compiler_params=pltpu.CompilerParams(vmem_limit_bytes=VMEM_BYTES),
        cost_estimate=pl.CostEstimate(flops=1, bytes_accessed=1, transcendentals=0),
    )(*args)


def together(*arrays, earlier=()):
    k = len(arrays)
    return pl.pallas_call(
        lambda *refs: None,
        out_shape=[jax.ShapeDtypeStruct(x.shape, x.dtype) for x in arrays],
        in_specs=[ANY] * (k + len(earlier)),
        out_specs=[ANY] * k,
        input_output_aliases={i: i for i in range(k)},
    )(*arrays, *earlier)


def square_plan(fields):
    n = N

    def move(x, target):
        pairs = []
        for f in range(fields):
            for r in range(n):
                for c in range(n):
                    to = target(r, c)
                    if to is not None and 0 <= to[0] < n:
                        pairs.append(((f * n + r) * n + c, (f * n + to[0]) * n + to[1]))
        return lax.ppermute(x, AXES, pairs)

    def up(x, s):
        return move(x, lambda r, c: (r + 1, c) if r >= s - 1 else None)

    def down(x, s):
        def target(r, c):
            k = r + s - 1
            return (r - 1, c) if k < n and c <= k else None

        return move(x, target)

    def on_device(root_inverse, child_inverse, panel, structure):
        h, w = panel.shape
        half = h // 2
        lower = lambda r, c: c <= r
        shape = jax.ShapeDtypeStruct
        dma = pltpu.SemaphoreType.DMA
        t_block, child_block = shape((w, h), BF16), shape((w, w), BF16)

        _, panel_kept = mask_panel(panel, structure)
        panel_1 = up(panel_kept, 1)
        root_across = move(root_inverse, lambda r, c: (r, c ^ 2) if lower(r, c) else None)
        below_1 = down(root_inverse, 1)
        (root_late,) = together(root_inverse, earlier=(panel_1,))
        root_beside = move(root_late, lambda r, c: (r, c ^ 1) if lower(r, c) else None)
        panel_2 = up(panel_1, 2)
        (panel_2,) = together(panel_2, earlier=(below_1, root_across, root_beside))
        (child_late,) = together(child_inverse, earlier=(root_across,))
        child_row = lax.all_gather(child_late, "col", axis=1, tiled=True)
        panel_3 = up(panel_2, 3)
        root_both = move(root_across, lambda r, c: (r, c ^ 1) if lower(r, c ^ 2) else None)
        below_2a = down(below_1[:half], 2)
        across_3 = move(root_across, lambda r, c: (0, 2) if (r, c) == (3, 2) else None)

        def to_across(x, rows):
            return move(x, lambda r, c: (r, c ^ 2) if r == c and r in rows else None)

        def to_beside(x, rows):
            return move(x, lambda r, c: (r, c ^ 1) if r == c and r in rows else None)

        def on_beside(x, rows):
            return move(x, lambda r, c: (r, c ^ 1) if r == c ^ 2 and r in rows else None)

        across_1 = to_across(below_1, (1, 2))

        root_row = (root_inverse, root_beside, root_across, root_both)
        panels = (panel_kept, panel_1, panel_2, panel_3)
        t, t_t, sent, below_1, below_2a = local_call(
            functools.partial(product_kernel, deps=2, gated=2),
            [ANY] * 8,
            [shape((h, w), BF16), t_block, t_block],
            [
                pltpu.VMEM((n, h, h), BF16),
                pltpu.VMEM((n, h, w), BF16),
                pltpu.VMEM((h, w), F32),
                dma((n,)),
                dma((n,)),
                dma,
            ],
            *root_row,
            *panels,
            across_1,
            across_3,
            below_1,
            below_2a,
            gated=2,
        )
        t_row = lax.all_gather(t, "col", axis=1, tiled=True)
        step = lambda x: move(x, lambda r, c: (r - 1, c))
        chain = [ANY] * 4 + [VMEM] * 2
        below_2b = came = move(sent, lambda r, c: (r - 1, c) if (r, c) != (1, 3) else None)
        beside_1 = to_beside(below_1, (0, 1, 2))
        far_1 = on_beside(across_1, (1, 2))
        own, below_2a = local_call(
            own_kernel,
            [ANY] * 4 + [VMEM],
            [shape((w, h), F32)],
            [pltpu.VMEM((h, h), BF16), dma],
            *root_row,
            t_t,
            below_2a,
            gated=1,
        )
        below_3a = down(below_2a, 3)
        (sent,) = local_call(
            functools.partial(chain_kernel, step=1, deps=3, gated=0),
            chain,
            [t_block],
            [pltpu.VMEM((h, h), BF16), dma],
            *root_row,
            t_t,
            came,
            own,
            far_1,
            beside_1,
        )
        below_2 = jnp.concatenate((below_2a, below_2b), 0)
        below_3b = came = step(sent)
        across_2 = to_across(below_2, (0, 1))
        beside_2 = to_beside(below_2, (0, 1))

        far_part, near_part, child_on, child_own = local_call(
            child_kernel,
            [VMEM] * 4,
            [child_block, child_block, shape((w, w), F32), shape((w, w), F32)],
            [pltpu.VMEM((w, w), BF16)],
            t_t,
            t_row,
            child_inverse,
            child_row,
            sent,
        )
        child_far = move(far_part, lambda r, c: (r ^ 1, c))
        child_near = move(near_part, lambda r, c: (r ^ 1, c))
        (root_sum,) = local_call(
            diagonal_kernel,
            [],
            [shape((h, h), F32)],
            [pltpu.VMEM((h, h), BF16), pltpu.VMEM((h, h), BF16), dma((2,))],
            *root_row,
            far_part,
        )
        sent, across_2, across_3, below_3a = local_call(
            functools.partial(chain_kernel, step=2, deps=3, gated=3),
            chain,
            [t_block],
            [pltpu.VMEM((h, h), BF16), dma],
            *root_row,
            t_t,
            came,
            child_far,
            child_near,
            beside_2,
            across_2,
            across_3,
            below_3a,
            gated=3,
        )
        came = step(sent)
        (child_onward,) = local_call(
            child_onward_kernel, [VMEM] * 2, [child_block], [], child_on, child_far, sent
        )
        child_last = move(child_onward, lambda r, c: (r ^ 2, c))
        below_3 = jnp.concatenate((below_3a, below_3b), 0)
        beside_3 = to_beside(below_3, (0,))
        far_2 = on_beside(across_2, (0, 1))
        far_3 = on_beside(across_3, (0,))
        (sigma_cross,) = local_call(
            cross_end_kernel,
            [SMEM] + [VMEM] * 2,
            [shape((h, w), BF16)],
            [],
            structure,
            own,
            came,
        )
        (sigma_root,) = local_call(
            root_kernel,
            [VMEM],
            [shape((h, h), BF16)],
            [
                pltpu.VMEM((h, h), F32),
                pltpu.VMEM((3, h, h), BF16),
                pltpu.VMEM((3, h, h), BF16),
                dma((3,)),
                dma((3,)),
            ],
            root_sum,
            below_1,
            below_2,
            below_3,
            beside_1,
            beside_2,
            beside_3,
            across_1,
            across_2,
            across_3,
            far_1,
            far_2,
            far_3,
        )
        (sigma_child,) = local_call(
            child_end_kernel,
            [VMEM] * 3,
            [shape((w, w), F32)],
            [],
            child_own,
            child_near,
            child_last,
            sigma_root,
        )
        return (sigma_root, sigma_cross, sigma_child)

    return on_device


def solution(mesh):
    square = mesh.shape["row"] == N and mesh.shape["col"] == N
    spec = P(("fields", "row"), "col")
    return jax.shard_map(
        square_plan(mesh.shape["fields"]) if square else gather_plan,
        mesh=mesh,
        in_specs=(spec, spec, spec, P(("fields", "row"))),
        out_specs=(spec, spec, spec),
        check_vma=False,
    )
```

```python
import functools

import jax
import jax.numpy as jnp
from jax import lax
from jax.experimental import pallas as pl
from jax.experimental.pallas import tpu as pltpu
from jax.sharding import PartitionSpec as P

BLOCK = 128
AXES = ("fields", "row", "col")
BF16 = jnp.bfloat16
F32 = jnp.float32
TILE = 256
N = 4
VMEM_BYTES = 40 * 1024 * 1024


def inner_dot(left_part, right_part):
    return lax.dot_general(
        left_part, right_part, (((0,), (0,)), ((), ())), preferred_element_type=F32
    )


def dot(a, b):
    return jnp.dot(a, b, preferred_element_type=F32)


def mask_panel(panel, structure):
    kept_rows = jnp.repeat(structure, BLOCK)[:, None] > 0
    return kept_rows, jnp.where(kept_rows, panel, jnp.zeros_like(panel))


def gather_plan(root_inverse, child_inverse, panel, structure):
    kept_rows, panel_kept = mask_panel(panel, structure)
    root_full, child_rows, panel_full = (
        lax.all_gather(root_inverse, "col", axis=1, tiled=True),
        lax.all_gather(child_inverse, "col", axis=1, tiled=True),
        lax.all_gather(panel_kept, "col", axis=1, tiled=True),
    )
    root_sum = lax.psum_scatter(
        inner_dot(root_full, root_inverse), "row", scatter_dimension=0, tiled=True
    )
    sigma_root = root_sum.astype(BF16)
    sigma_rows = lax.all_gather(sigma_root, "col", axis=1, tiled=True)
    cross_sum = jnp.dot(
        sigma_rows,
        lax.all_gather(panel_kept, "row", axis=0, tiled=True),
        preferred_element_type=F32,
    )
    sigma_cross = jnp.where(kept_rows, -cross_sum, jnp.zeros_like(cross_sum)).astype(BF16)
    sigma_child = lax.psum_scatter(
        (inner_dot(child_rows, child_inverse) - inner_dot(panel_full, sigma_cross)).astype(BF16),
        "row",
        scatter_dimension=0,
        tiled=True,
    ).astype(F32)
    return (sigma_root, sigma_cross, sigma_child)


def position():
    return lax.axis_index("row"), lax.axis_index("col")


def start(src, dst, sem):
    pltpu.make_async_copy(src, dst, sem).start()


def wait(src, dst, sem):
    pltpu.make_async_copy(src, dst, sem).wait()


def start_picked(refs, index, dst, sem):
    for m, ref in enumerate(refs):

        @pl.when(index == m)
        def _():
            start(ref, dst, sem)


def tile(i):
    return pl.ds(pl.multiple_of(i * TILE, TILE), TILE)


def product_kernel(l0, l1, l2, l3, p0, p1, p2, p3, *refs, deps, gated):
    below = refs[0]
    t_ref, tt_ref, sent_ref = refs[deps + gated : deps + gated + 3]
    rows, panels, acc, row_sems, panel_sems, sem = refs[deps + 2 * gated + 3 :]
    r, c = position()
    half = below.at[sent_ref.shape[0] :]

    @pl.when((r == 1) | (r == 2))
    def _():
        start(half, sent_ref, sem)

    for m, ref in enumerate((l0, l1, l2, l3)):
        j = c ^ m

        @pl.when(j <= r)
        def _():
            start(ref, rows.at[r - j], row_sems.at[r - j])

    for s, ref in enumerate((p0, p1, p2, p3)):

        @pl.when(s <= r)
        def _():
            start(ref, panels.at[s], panel_sems.at[s])

    for s in range(N):

        @pl.when(s <= r)
        def _():
            wait(l0, rows.at[s], row_sems.at[s])
            wait(p0, panels.at[s], panel_sems.at[s])

            @pl.loop(0, acc.shape[0] // TILE)
            def _(i):
                term = dot(rows[s, tile(i), :], panels[s])
                if s > 0:
                    term = term + acc[tile(i), :]
                acc[tile(i), :] = term

    @pl.loop(0, acc.shape[0] // TILE)
    def _(i):
        value = acc[tile(i), :]
        t_ref[tile(i), :] = value.astype(BF16)
        tt_ref[:, tile(i)] = value.T.astype(BF16)

    @pl.when(r == 3)
    def _():
        @pl.loop(0, tt_ref.shape[0] // TILE)
        def _(i):
            sent_ref[tile(i), :] = dot(tt_ref[tile(i), :], rows[3]).astype(BF16)

    @pl.when((r == 1) | (r == 2))
    def _():
        wait(half, sent_ref, sem)


def own_kernel(l0, l1, l2, l3, tt_ref, _in0, _in1, _in2, own_ref, _out0, _out1, _out2, block, sem):
    r, c = position()
    start_picked((l0, l1, l2, l3), r ^ c, block, sem)
    wait(l0, block, sem)

    @pl.loop(0, tt_ref.shape[0] // TILE)
    def _(i):
        own_ref[tile(i), :] = dot(tt_ref[tile(i), :], block[...])


def chain_kernel(l0, l1, l2, l3, tt_ref, came_ref, *refs, step, deps, gated):
    sent_ref = refs[deps + gated]
    block, sem = refs[deps + 2 * gated + 1 :]
    r, c = position()
    i = step + r - 3

    @pl.when(i >= 0)
    def _():
        start_picked((l0, l1, l2, l3), i ^ c, block, sem)
        wait(l0, block, sem)

        @pl.when(r == 3)
        def _():
            @pl.loop(0, tt_ref.shape[0] // TILE)
            def _(j):
                sent_ref[tile(j), :] = dot(tt_ref[tile(j), :], block[...]).astype(BF16)

        @pl.when(r < 3)
        def _():
            @pl.loop(0, tt_ref.shape[0] // TILE)
            def _(j):
                term = dot(tt_ref[tile(j), :], block[...])
                sent_ref[tile(j), :] = (term + came_ref[tile(j), :].astype(F32)).astype(BF16)

    @pl.when((i < 0) & (r == 1))
    def _():
        sent_ref[...] = came_ref[...]


def child_kernel(
    tt_ref, t_row_ref, child_ref, child_row_ref, _dep, far_ref, near_ref, onward_ref, own_ref, child_t
):
    r, _ = position()
    w = child_ref.shape[1]
    child_t[...] = child_ref[...].astype(F32).T.astype(BF16)
    for flip, ref in ((3, far_ref), (1, near_ref), (2, onward_ref), (0, own_ref)):
        columns = pl.ds(pl.multiple_of((r ^ flip) * w, w), w)

        @pl.loop(0, w // TILE)
        def _(i):
            term = dot(tt_ref[tile(i), :], t_row_ref[:, columns])
            term = term + dot(child_t[tile(i), :], child_row_ref[:, columns])
            ref[tile(i), :] = term.astype(ref.dtype)


def child_onward_kernel(own_ref, far_ref, _dep, out_ref):
    out_ref[...] = (own_ref[...] + far_ref[...].astype(F32)).astype(BF16)


def diagonal_kernel(l0, l1, l2, l3, _dep, acc_ref, left, held, sems):
    r, c = position()

    @pl.when(c <= r)
    def _():
        start_picked((l0, l1, l2, l3), r ^ c, left, sems.at[0])
        start(l0, held, sems.at[1])
        wait(l0, left, sems.at[0])
        wait(l0, held, sems.at[1])

        @pl.loop(0, acc_ref.shape[0] // TILE)
        def _(i):
            acc_ref[tile(i), :] = inner_dot(left[:, tile(i)], held[...])

    @pl.when(c > r)
    def _():
        acc_ref[...] = jnp.zeros_like(acc_ref)


def root_kernel(acc_ref, h1, h2, h3, b1, b2, b3, x1, x2, x3, f1, f2, f3, out_ref, acc, left, held, left_sems, held_sems):
    r, c = position()
    refs = ((h1, b1, x1, f1), (h2, b2, x2, f2), (h3, b3, x3, f3))
    needed = [(r + s < N) & (c <= r + s) for s in (1, 2, 3)]
    for s, places in enumerate(refs):

        @pl.when(needed[s])
        def _():
            start_picked(places, r ^ c, left.at[s], left_sems.at[s])
            start(places[0], held.at[s], held_sems.at[s])

    acc[...] = acc_ref[...]
    for s in range(3):

        @pl.when(needed[s])
        def _():
            wait(h1, left.at[s], left_sems.at[s])
            wait(h1, held.at[s], held_sems.at[s])

            @pl.loop(0, acc.shape[0] // TILE)
            def _(i):
                acc[tile(i), :] += inner_dot(left[s, :, tile(i)], held[s])

    out_ref[...] = acc[...].astype(BF16)


def cross_end_kernel(structure, own_ref, came_ref, _dep, out_ref):
    for b in range(own_ref.shape[1] // BLOCK):
        rows = slice(b * BLOCK, (b + 1) * BLOCK)
        total = own_ref[:, rows] + came_ref[:, rows].astype(F32)
        kept = structure[b] > 0
        out_ref[rows, :] = jnp.where(kept, -total.T, jnp.zeros_like(total.T)).astype(BF16)


def child_end_kernel(own_ref, near_ref, last_ref, _dep, out_ref):
    total = own_ref[...] + near_ref[...].astype(F32) + last_ref[...].astype(F32)
    out_ref[...] = total.T


ANY = pl.BlockSpec(memory_space=pl.ANY)
VMEM = pl.BlockSpec(memory_space=pltpu.VMEM)
SMEM = pl.BlockSpec(memory_space=pltpu.SMEM)


def local_call(kernel, in_specs, outs, scratch, *args, gated=0, out_specs=None):
    first = len(args) - gated
    outs = outs + [jax.ShapeDtypeStruct(x.shape, x.dtype) for x in args[first:]]
    return pl.pallas_call(
        kernel,
        out_shape=outs,
        in_specs=in_specs + [ANY] * (len(args) - len(in_specs)),
        out_specs=(out_specs or [VMEM] * (len(outs) - gated)) + [ANY] * gated,
        scratch_shapes=scratch,
        input_output_aliases={first + i: len(outs) - gated + i for i in range(gated)},
        compiler_params=pltpu.CompilerParams(vmem_limit_bytes=VMEM_BYTES),
        cost_estimate=pl.CostEstimate(flops=1, bytes_accessed=1, transcendentals=0),
    )(*args)


def together(*arrays, earlier=()):
    k = len(arrays)
    return pl.pallas_call(
        lambda *refs: None,
        out_shape=[jax.ShapeDtypeStruct(x.shape, x.dtype) for x in arrays],
        in_specs=[ANY] * (k + len(earlier)),
        out_specs=[ANY] * k,
        input_output_aliases={i: i for i in range(k)},
    )(*arrays, *earlier)


def square_plan(fields):
    n = N

    def move(x, target):
        pairs = []
        for f in range(fields):
            for r in range(n):
                for c in range(n):
                    to = target(r, c)
                    if to is not None and 0 <= to[0] < n:
                        pairs.append(((f * n + r) * n + c, (f * n + to[0]) * n + to[1]))
        return lax.ppermute(x, AXES, pairs)

    def up(x, s):
        return move(x, lambda r, c: (r + 1, c) if r >= s - 1 else None)

    def down(x, s):
        def target(r, c):
            k = r + s - 1
            return (r - 1, c) if k < n and c <= k else None

        return move(x, target)

    def on_device(root_inverse, child_inverse, panel, structure):
        h, w = panel.shape
        half = h // 2
        lower = lambda r, c: c <= r
        shape = jax.ShapeDtypeStruct
        dma = pltpu.SemaphoreType.DMA
        t_block, child_block = shape((w, h), BF16), shape((w, w), BF16)

        _, panel_kept = mask_panel(panel, structure)
        panel_1 = up(panel_kept, 1)
        root_across = move(root_inverse, lambda r, c: (r, c ^ 2) if lower(r, c) else None)
        below_1 = down(root_inverse, 1)
        (root_late,) = together(root_inverse, earlier=(panel_1,))
        root_beside = move(root_late, lambda r, c: (r, c ^ 1) if lower(r, c) else None)
        panel_2 = up(panel_1, 2)
        panel_2, child_late = together(
            panel_2, child_inverse, earlier=(below_1, root_across, root_beside)
        )
        child_row = lax.all_gather(child_late, "col", axis=1, tiled=True)
        panel_3 = up(panel_2, 3)
        root_both = move(root_across, lambda r, c: (r, c ^ 1) if lower(r, c ^ 2) else None)
        below_2a = down(below_1[:half], 2)
        across_3 = move(root_across, lambda r, c: (0, 2) if (r, c) == (3, 2) else None)

        def to_across(x, rows):
            return move(x, lambda r, c: (r, c ^ 2) if r == c and r in rows else None)

        def to_beside(x, rows):
            return move(x, lambda r, c: (r, c ^ 1) if r == c and r in rows else None)

        def on_beside(x, rows):
            return move(x, lambda r, c: (r, c ^ 1) if r == c ^ 2 and r in rows else None)

        across_1 = to_across(below_1, (1, 2))

        root_row = (root_inverse, root_beside, root_across, root_both)
        panels = (panel_kept, panel_1, panel_2, panel_3)
        t, t_t, sent = local_call(
            functools.partial(product_kernel, deps=4, gated=0),
            [ANY] * 8,
            [shape((h, w), BF16), t_block, t_block],
            [
                pltpu.VMEM((n, h, h), BF16),
                pltpu.VMEM((n, h, w), BF16),
                pltpu.VMEM((h, w), F32),
                dma((n,)),
                dma((n,)),
                dma,
            ],
            *root_row,
            *panels,
            below_1,
            across_1,
            across_3,
            below_2a,
        )
        t_row = lax.all_gather(t, "col", axis=1, tiled=True)
        step = lambda x: move(x, lambda r, c: (r - 1, c))
        chain = [ANY] * 4 + [VMEM] * 2
        below_2b = came = move(sent, lambda r, c: (r - 1, c) if (r, c) != (1, 3) else None)
        far_1 = on_beside(across_1, (1, 2))
        own, below_1, below_2a, across_3 = local_call(
            own_kernel,
            [ANY] * 4 + [VMEM],
            [shape((w, h), F32)],
            [pltpu.VMEM((h, h), BF16), dma],
            *root_row,
            t_t,
            below_1,
            below_2a,
            across_3,
            gated=3,
        )
        far_3 = on_beside(across_3, (0,))
        below_3a = down(below_2a, 3)
        beside_1 = to_beside(below_1, (0, 1, 2))
        (sent,) = local_call(
            functools.partial(chain_kernel, step=1, deps=3, gated=0),
            chain,
            [t_block],
            [pltpu.VMEM((h, h), BF16), dma],
            *root_row,
            t_t,
            came,
            far_3,
            far_1,
            beside_1,
        )
        below_2 = jnp.concatenate((below_2a, below_2b), 0)
        below_3b = came = step(sent)
        across_2 = to_across(below_2, (0, 1))
        beside_2 = to_beside(below_2, (0, 1))

        far_part, near_part, child_on, child_own = local_call(
            child_kernel,
            [VMEM] * 4,
            [child_block, child_block, shape((w, w), F32), shape((w, w), F32)],
            [pltpu.VMEM((w, w), BF16)],
            t_t,
            t_row,
            child_inverse,
            child_row,
            sent,
        )
        child_far = move(far_part, lambda r, c: (r ^ 1, c))
        (root_sum,) = local_call(
            diagonal_kernel,
            [],
            [shape((h, h), F32)],
            [pltpu.VMEM((h, h), BF16), pltpu.VMEM((h, h), BF16), dma((2,))],
            *root_row,
            far_part,
        )
        sent, across_2, below_3a = local_call(
            functools.partial(chain_kernel, step=2, deps=2, gated=2),
            chain,
            [t_block],
            [pltpu.VMEM((h, h), BF16), dma],
            *root_row,
            t_t,
            came,
            child_far,
            beside_2,
            across_2,
            below_3a,
            gated=2,
        )
        came = step(sent)
        (child_onward,) = local_call(
            child_onward_kernel, [VMEM] * 2, [child_block], [], child_on, child_far, sent
        )
        child_near = move(near_part, lambda r, c: (r ^ 1, c))
        child_last = move(child_onward, lambda r, c: (r ^ 2, c))
        below_3 = jnp.concatenate((below_3a, below_3b), 0)
        beside_3 = to_beside(below_3, (0,))
        far_2 = on_beside(across_2, (0, 1))
        (sigma_root,) = local_call(
            root_kernel,
            [VMEM],
            [shape((h, h), BF16)],
            [
                pltpu.VMEM((h, h), F32),
                pltpu.VMEM((3, h, h), BF16),
                pltpu.VMEM((3, h, h), BF16),
                dma((3,)),
                dma((3,)),
            ],
            root_sum,
            below_1,
            below_2,
            below_3,
            beside_1,
            beside_2,
            beside_3,
            across_1,
            across_2,
            across_3,
            far_1,
            far_2,
            far_3,
        )
        (sigma_cross,) = local_call(
            cross_end_kernel,
            [SMEM] + [VMEM] * 2,
            [shape((h, w), BF16)],
            [],
            structure,
            own,
            came,
            sigma_root,
        )
        (sigma_child,) = local_call(
            child_end_kernel,
            [VMEM] * 3,
            [shape((w, w), F32)],
            [],
            child_own,
            child_near,
            child_last,
            sigma_cross,
        )
        return (sigma_root, sigma_cross, sigma_child)

    return on_device


def solution(mesh):
    square = mesh.shape["row"] == N and mesh.shape["col"] == N
    spec = P(("fields", "row"), "col")
    return jax.shard_map(
        square_plan(mesh.shape["fields"]) if square else gather_plan,
        mesh=mesh,
        in_specs=(spec, spec, spec, P(("fields", "row"))),
        out_specs=(spec, spec, spec),
        check_vma=False,
    )
```

```python
import functools

import jax
import jax.numpy as jnp
from jax import lax
from jax.experimental import pallas as pl
from jax.experimental.pallas import tpu as pltpu
from jax.sharding import PartitionSpec as P

BLOCK = 128
AXES = ("fields", "row", "col")
BF16 = jnp.bfloat16
F32 = jnp.float32
TILE = 256
N = 4
VMEM_BYTES = 40 * 1024 * 1024


def inner_dot(left_part, right_part):
    return lax.dot_general(
        left_part, right_part, (((0,), (0,)), ((), ())), preferred_element_type=F32
    )


def dot(a, b):
    return jnp.dot(a, b, preferred_element_type=F32)


def mask_panel(panel, structure):
    kept_rows = jnp.repeat(structure, BLOCK)[:, None] > 0
    return kept_rows, jnp.where(kept_rows, panel, jnp.zeros_like(panel))


def gather_plan(root_inverse, child_inverse, panel, structure):
    kept_rows, panel_kept = mask_panel(panel, structure)
    root_full, child_rows, panel_full = (
        lax.all_gather(root_inverse, "col", axis=1, tiled=True),
        lax.all_gather(child_inverse, "col", axis=1, tiled=True),
        lax.all_gather(panel_kept, "col", axis=1, tiled=True),
    )
    root_sum = lax.psum_scatter(
        inner_dot(root_full, root_inverse), "row", scatter_dimension=0, tiled=True
    )
    sigma_root = root_sum.astype(BF16)
    sigma_rows = lax.all_gather(sigma_root, "col", axis=1, tiled=True)
    cross_sum = jnp.dot(
        sigma_rows,
        lax.all_gather(panel_kept, "row", axis=0, tiled=True),
        preferred_element_type=F32,
    )
    sigma_cross = jnp.where(kept_rows, -cross_sum, jnp.zeros_like(cross_sum)).astype(BF16)
    sigma_child = lax.psum_scatter(
        (inner_dot(child_rows, child_inverse) - inner_dot(panel_full, sigma_cross)).astype(BF16),
        "row",
        scatter_dimension=0,
        tiled=True,
    ).astype(F32)
    return (sigma_root, sigma_cross, sigma_child)


def position():
    return lax.axis_index("row"), lax.axis_index("col")


def start(src, dst, sem):
    pltpu.make_async_copy(src, dst, sem).start()


def wait(src, dst, sem):
    pltpu.make_async_copy(src, dst, sem).wait()


def start_picked(refs, index, dst, sem):
    for m, ref in enumerate(refs):

        @pl.when(index == m)
        def _():
            start(ref, dst, sem)


def tile(i):
    return pl.ds(pl.multiple_of(i * TILE, TILE), TILE)


def product_kernel(l0, l1, l2, l3, p0, p1, p2, acc_ref, rows, panels, row_sems, panel_sems):
    r, c = position()
    for m, ref in enumerate((l0, l1, l2, l3)):
        j = c ^ m

        @pl.when((j <= r) & (r - j < 3))
        def _():
            start(ref, rows.at[r - j], row_sems.at[r - j])

    for s, ref in enumerate((p0, p1, p2)):

        @pl.when(s <= r)
        def _():
            start(ref, panels.at[s], panel_sems.at[s])

    for s in range(3):

        @pl.when(s <= r)
        def _():
            wait(l0, rows.at[s], row_sems.at[s])
            wait(p0, panels.at[s], panel_sems.at[s])

            @pl.loop(0, acc_ref.shape[0] // TILE)
            def _(i):
                term = dot(rows[s, tile(i), :], panels[s])
                if s > 0:
                    term = term + acc_ref[tile(i), :]
                acc_ref[tile(i), :] = term


def product_end_kernel(l0, l1, l2, l3, acc_ref, p3_ref, *refs, deps, gated):
    below = refs[0]
    t_ref, tt_ref, sent_ref = refs[deps + gated : deps + gated + 3]
    block, block_sem, sem = refs[deps + 2 * gated + 3 :]
    r, c = position()
    half = below.at[sent_ref.shape[0] :]

    @pl.when((r == 1) | (r == 2))
    def _():
        start(half, sent_ref, sem)

    def finish(i, value):
        t_ref[tile(i), :] = value.astype(BF16)
        tt_ref[:, tile(i)] = value.T.astype(BF16)

    @pl.when(r < 3)
    def _():
        @pl.loop(0, acc_ref.shape[0] // TILE)
        def _(i):
            finish(i, acc_ref[tile(i), :])

    @pl.when(r == 3)
    def _():
        start_picked((l0, l1, l2, l3), c, block, block_sem)
        wait(l0, block, block_sem)

        @pl.loop(0, acc_ref.shape[0] // TILE)
        def _(i):
            finish(i, dot(block[tile(i), :], p3_ref[...]) + acc_ref[tile(i), :])

        @pl.loop(0, tt_ref.shape[0] // TILE)
        def _(i):
            sent_ref[tile(i), :] = dot(tt_ref[tile(i), :], block[...]).astype(BF16)

    @pl.when((r == 1) | (r == 2))
    def _():
        wait(half, sent_ref, sem)


def own_kernel(l0, l1, l2, l3, tt_ref, _in0, _in1, _in2, own_ref, _out0, _out1, _out2, block, sem):
    r, c = position()
    start_picked((l0, l1, l2, l3), r ^ c, block, sem)
    wait(l0, block, sem)

    @pl.loop(0, tt_ref.shape[0] // TILE)
    def _(i):
        own_ref[tile(i), :] = dot(tt_ref[tile(i), :], block[...])


def chain_kernel(l0, l1, l2, l3, tt_ref, came_ref, *refs, step, deps, gated):
    sent_ref = refs[deps + gated]
    block, sem = refs[deps + 2 * gated + 1 :]
    r, c = position()
    i = step + r - 3

    @pl.when(i >= 0)
    def _():
        start_picked((l0, l1, l2, l3), i ^ c, block, sem)
        wait(l0, block, sem)

        @pl.when(r == 3)
        def _():
            @pl.loop(0, tt_ref.shape[0] // TILE)
            def _(j):
                sent_ref[tile(j), :] = dot(tt_ref[tile(j), :], block[...]).astype(BF16)

        @pl.when(r < 3)
        def _():
            @pl.loop(0, tt_ref.shape[0] // TILE)
            def _(j):
                term = dot(tt_ref[tile(j), :], block[...])
                sent_ref[tile(j), :] = (term + came_ref[tile(j), :].astype(F32)).astype(BF16)

    @pl.when((i < 0) & (r == 1))
    def _():
        sent_ref[...] = came_ref[...]


def child_kernel(
    tt_ref, t_row_ref, child_ref, child_row_ref, _dep, far_ref, near_ref, onward_ref, own_ref, child_t
):
    r, _ = position()
    w = child_ref.shape[1]
    child_t[...] = child_ref[...].astype(F32).T.astype(BF16)
    for flip, ref in ((3, far_ref), (1, near_ref), (2, onward_ref), (0, own_ref)):
        columns = pl.ds(pl.multiple_of((r ^ flip) * w, w), w)

        @pl.loop(0, w // TILE)
        def _(i):
            term = dot(tt_ref[tile(i), :], t_row_ref[:, columns])
            term = term + dot(child_t[tile(i), :], child_row_ref[:, columns])
            ref[tile(i), :] = term.astype(ref.dtype)


def child_onward_kernel(own_ref, far_ref, _dep, out_ref):
    out_ref[...] = (own_ref[...] + far_ref[...].astype(F32)).astype(BF16)


def diagonal_kernel(l0, l1, l2, l3, _dep, acc_ref, left, held, sems):
    r, c = position()

    @pl.when(c <= r)
    def _():
        start_picked((l0, l1, l2, l3), r ^ c, left, sems.at[0])
        start(l0, held, sems.at[1])
        wait(l0, left, sems.at[0])
        wait(l0, held, sems.at[1])

        @pl.loop(0, acc_ref.shape[0] // TILE)
        def _(i):
            acc_ref[tile(i), :] = inner_dot(left[:, tile(i)], held[...])

    @pl.when(c > r)
    def _():
        acc_ref[...] = jnp.zeros_like(acc_ref)


def root_kernel(acc_ref, h1, h2, h3, b1, b2, b3, x1, x2, x3, f1, f2, f3, out_ref, acc, left, held, left_sems, held_sems):
    r, c = position()
    refs = ((h1, b1, x1, f1), (h2, b2, x2, f2), (h3, b3, x3, f3))
    needed = [(r + s < N) & (c <= r + s) for s in (1, 2, 3)]
    for s, places in enumerate(refs):

        @pl.when(needed[s])
        def _():
            start_picked(places, r ^ c, left.at[s], left_sems.at[s])
            start(places[0], held.at[s], held_sems.at[s])

    acc[...] = acc_ref[...]
    for s in range(3):

        @pl.when(needed[s])
        def _():
            wait(h1, left.at[s], left_sems.at[s])
            wait(h1, held.at[s], held_sems.at[s])

            @pl.loop(0, acc.shape[0] // TILE)
            def _(i):
                acc[tile(i), :] += inner_dot(left[s, :, tile(i)], held[s])

    out_ref[...] = acc[...].astype(BF16)


def cross_end_kernel(structure, own_ref, came_ref, _dep, out_ref):
    for b in range(own_ref.shape[1] // BLOCK):
        rows = slice(b * BLOCK, (b + 1) * BLOCK)
        total = own_ref[:, rows] + came_ref[:, rows].astype(F32)
        kept = structure[b] > 0
        out_ref[rows, :] = jnp.where(kept, -total.T, jnp.zeros_like(total.T)).astype(BF16)


def child_end_kernel(own_ref, near_ref, last_ref, _dep, out_ref):
    total = own_ref[...] + near_ref[...].astype(F32) + last_ref[...].astype(F32)
    out_ref[...] = total.T


ANY = pl.BlockSpec(memory_space=pl.ANY)
VMEM = pl.BlockSpec(memory_space=pltpu.VMEM)
SMEM = pl.BlockSpec(memory_space=pltpu.SMEM)


def local_call(kernel, in_specs, outs, scratch, *args, gated=0, out_specs=None):
    first = len(args) - gated
    outs = outs + [jax.ShapeDtypeStruct(x.shape, x.dtype) for x in args[first:]]
    return pl.pallas_call(
        kernel,
        out_shape=outs,
        in_specs=in_specs + [ANY] * (len(args) - len(in_specs)),
        out_specs=(out_specs or [VMEM] * (len(outs) - gated)) + [ANY] * gated,
        scratch_shapes=scratch,
        input_output_aliases={first + i: len(outs) - gated + i for i in range(gated)},
        compiler_params=pltpu.CompilerParams(vmem_limit_bytes=VMEM_BYTES),
        cost_estimate=pl.CostEstimate(flops=1, bytes_accessed=1, transcendentals=0),
    )(*args)


def together(*arrays, earlier=()):
    k = len(arrays)
    return pl.pallas_call(
        lambda *refs: None,
        out_shape=[jax.ShapeDtypeStruct(x.shape, x.dtype) for x in arrays],
        in_specs=[ANY] * (k + len(earlier)),
        out_specs=[ANY] * k,
        input_output_aliases={i: i for i in range(k)},
    )(*arrays, *earlier)


def square_plan(fields):
    n = N

    def move(x, target):
        pairs = []
        for f in range(fields):
            for r in range(n):
                for c in range(n):
                    to = target(r, c)
                    if to is not None and 0 <= to[0] < n:
                        pairs.append(((f * n + r) * n + c, (f * n + to[0]) * n + to[1]))
        return lax.ppermute(x, AXES, pairs)

    def up(x, s):
        return move(x, lambda r, c: (r + 1, c) if r >= s - 1 else None)

    def down(x, s):
        def target(r, c):
            k = r + s - 1
            return (r - 1, c) if k < n and c <= k else None

        return move(x, target)

    def on_device(root_inverse, child_inverse, panel, structure):
        h, w = panel.shape
        half = h // 2
        lower = lambda r, c: c <= r
        shape = jax.ShapeDtypeStruct
        dma = pltpu.SemaphoreType.DMA
        t_block, child_block = shape((w, h), BF16), shape((w, w), BF16)

        _, panel_kept = mask_panel(panel, structure)
        panel_1 = up(panel_kept, 1)
        root_across = move(root_inverse, lambda r, c: (r, c ^ 2) if lower(r, c) else None)
        below_1 = down(root_inverse, 1)
        (root_late,) = together(root_inverse, earlier=(panel_1,))
        root_beside = move(root_late, lambda r, c: (r, c ^ 1) if lower(r, c) else None)
        panel_2 = up(panel_1, 2)
        panel_2, child_late = together(
            panel_2, child_inverse, earlier=(below_1, root_across, root_beside)
        )
        child_row = lax.all_gather(child_late, "col", axis=1, tiled=True)
        panel_3 = up(panel_2, 3)
        root_both = move(root_across, lambda r, c: (r, c ^ 1) if lower(r, c ^ 2) else None)
        below_2a = down(below_1[:half], 2)
        across_3 = move(root_across, lambda r, c: (0, 2) if (r, c) == (3, 2) else None)

        def to_across(x, rows):
            return move(x, lambda r, c: (r, c ^ 2) if r == c and r in rows else None)

        def to_beside(x, rows):
            return move(x, lambda r, c: (r, c ^ 1) if r == c and r in rows else None)

        def on_beside(x, rows):
            return move(x, lambda r, c: (r, c ^ 1) if r == c ^ 2 and r in rows else None)

        across_1 = to_across(below_1, (1, 2))

        root_row = (root_inverse, root_beside, root_across, root_both)
        panels = (panel_kept, panel_1, panel_2, panel_3)
        (t_sum,) = local_call(
            product_kernel,
            [ANY] * 7,
            [shape((h, w), F32)],
            [pltpu.VMEM((3, h, h), BF16), pltpu.VMEM((3, h, w), BF16), dma((3,)), dma((3,))],
            *root_row,
            *panels[:3],
        )
        t, t_t, sent = local_call(
            functools.partial(product_end_kernel, deps=4, gated=0),
            [ANY] * 4 + [VMEM] * 2,
            [shape((h, w), BF16), t_block, t_block],
            [pltpu.VMEM((h, h), BF16), dma, dma],
            *root_row,
            t_sum,
            panel_3,
            below_1,
            across_1,
            across_3,
            below_2a,
        )
        t_row = lax.all_gather(t, "col", axis=1, tiled=True)
        step = lambda x: move(x, lambda r, c: (r - 1, c))
        chain = [ANY] * 4 + [VMEM] * 2
        below_2b = came = move(sent, lambda r, c: (r - 1, c) if (r, c) != (1, 3) else None)
        far_1 = on_beside(across_1, (1, 2))
        own, below_1, below_2a, across_3 = local_call(
            own_kernel,
            [ANY] * 4 + [VMEM],
            [shape((w, h), F32)],
            [pltpu.VMEM((h, h), BF16), dma],
            *root_row,
            t_t,
            below_1,
            below_2a,
            across_3,
            gated=3,
        )
        far_3 = on_beside(across_3, (0,))
        below_3a = down(below_2a, 3)
        beside_1 = to_beside(below_1, (0, 1, 2))
        (sent,) = local_call(
            functools.partial(chain_kernel, step=1, deps=4, gated=0),
            chain,
            [t_block],
            [pltpu.VMEM((h, h), BF16), dma],
            *root_row,
            t_t,
            came,
            far_3,
            far_1,
            beside_1,
            below_3a,
        )
        below_2 = jnp.concatenate((below_2a, below_2b), 0)
        below_3b = came = step(sent)
        across_2 = to_across(below_2, (0, 1))
        beside_2 = to_beside(below_2, (0, 1))

        far_part, near_part, child_on, child_own = local_call(
            child_kernel,
            [VMEM] * 4,
            [child_block, child_block, shape((w, w), F32), shape((w, w), F32)],
            [pltpu.VMEM((w, w), BF16)],
            t_t,
            t_row,
            child_inverse,
            child_row,
            sent,
        )
        child_far = move(far_part, lambda r, c: (r ^ 1, c))
        child_near = move(near_part, lambda r, c: (r ^ 1, c))
        (root_sum,) = local_call(
            diagonal_kernel,
            [],
            [shape((h, h), F32)],
            [pltpu.VMEM((h, h), BF16), pltpu.VMEM((h, h), BF16), dma((2,))],
            *root_row,
            far_part,
        )
        sent, across_2, below_3a = local_call(
            functools.partial(chain_kernel, step=2, deps=3, gated=2),
            chain,
            [t_block],
            [pltpu.VMEM((h, h), BF16), dma],
            *root_row,
            t_t,
            came,
            child_far,
            child_near,
            beside_2,
            across_2,
            below_3a,
            gated=2,
        )
        came = step(sent)
        (child_onward,) = local_call(
            child_onward_kernel, [VMEM] * 2, [child_block], [], child_on, child_far, sent
        )
        child_last = move(child_onward, lambda r, c: (r ^ 2, c))
        below_3 = jnp.concatenate((below_3a, below_3b), 0)
        beside_3 = to_beside(below_3, (0,))
        far_2 = on_beside(across_2, (0, 1))
        (sigma_root,) = local_call(
            root_kernel,
            [VMEM],
            [shape((h, h), BF16)],
            [
                pltpu.VMEM((h, h), F32),
                pltpu.VMEM((3, h, h), BF16),
                pltpu.VMEM((3, h, h), BF16),
                dma((3,)),
                dma((3,)),
            ],
            root_sum,
            below_1,
            below_2,
            below_3,
            beside_1,
            beside_2,
            beside_3,
            across_1,
            across_2,
            across_3,
            far_1,
            far_2,
            far_3,
        )
        (sigma_cross,) = local_call(
            cross_end_kernel,
            [SMEM] + [VMEM] * 2,
            [shape((h, w), BF16)],
            [],
            structure,
            own,
            came,
            sigma_root,
        )
        (sigma_child,) = local_call(
            child_end_kernel,
            [VMEM] * 3,
            [shape((w, w), F32)],
            [],
            child_own,
            child_near,
            child_last,
            sigma_cross,
        )
        return (sigma_root, sigma_cross, sigma_child)

    return on_device


def solution(mesh):
    square = mesh.shape["row"] == N and mesh.shape["col"] == N
    spec = P(("fields", "row"), "col")
    return jax.shard_map(
        square_plan(mesh.shape["fields"]) if square else gather_plan,
        mesh=mesh,
        in_specs=(spec, spec, spec, P(("fields", "row"))),
        out_specs=(spec, spec, spec),
        check_vma=False,
    )
```

```python
import functools

import jax
import jax.numpy as jnp
from jax import lax
from jax.experimental import pallas as pl
from jax.experimental.pallas import tpu as pltpu
from jax.sharding import PartitionSpec as P

BLOCK = 128
AXES = ("fields", "row", "col")
BF16 = jnp.bfloat16
F32 = jnp.float32
TILE = 256
N = 4
VMEM_BYTES = 40 * 1024 * 1024


def inner_dot(left_part, right_part):
    return lax.dot_general(
        left_part, right_part, (((0,), (0,)), ((), ())), preferred_element_type=F32
    )


def dot(a, b):
    return jnp.dot(a, b, preferred_element_type=F32)


def mask_panel(panel, structure):
    kept_rows = jnp.repeat(structure, BLOCK)[:, None] > 0
    return kept_rows, jnp.where(kept_rows, panel, jnp.zeros_like(panel))


def gather_plan(root_inverse, child_inverse, panel, structure):
    kept_rows, panel_kept = mask_panel(panel, structure)
    root_full, child_rows, panel_full = (
        lax.all_gather(root_inverse, "col", axis=1, tiled=True),
        lax.all_gather(child_inverse, "col", axis=1, tiled=True),
        lax.all_gather(panel_kept, "col", axis=1, tiled=True),
    )
    root_sum = lax.psum_scatter(
        inner_dot(root_full, root_inverse), "row", scatter_dimension=0, tiled=True
    )
    sigma_root = root_sum.astype(BF16)
    sigma_rows = lax.all_gather(sigma_root, "col", axis=1, tiled=True)
    cross_sum = jnp.dot(
        sigma_rows,
        lax.all_gather(panel_kept, "row", axis=0, tiled=True),
        preferred_element_type=F32,
    )
    sigma_cross = jnp.where(kept_rows, -cross_sum, jnp.zeros_like(cross_sum)).astype(BF16)
    sigma_child = lax.psum_scatter(
        (inner_dot(child_rows, child_inverse) - inner_dot(panel_full, sigma_cross)).astype(BF16),
        "row",
        scatter_dimension=0,
        tiled=True,
    ).astype(F32)
    return (sigma_root, sigma_cross, sigma_child)


def position():
    return lax.axis_index("row"), lax.axis_index("col")


def start(src, dst, sem):
    pltpu.make_async_copy(src, dst, sem).start()


def wait(src, dst, sem):
    pltpu.make_async_copy(src, dst, sem).wait()


def start_picked(refs, index, dst, sem):
    for m, ref in enumerate(refs):

        @pl.when(index == m)
        def _():
            start(ref, dst, sem)


def tile(i):
    return pl.ds(pl.multiple_of(i * TILE, TILE), TILE)


def product_kernel(l0, l1, l2, l3, p0, p1, p2, acc_ref, rows, panels, row_sems, panel_sems):
    r, c = position()
    for m, ref in enumerate((l0, l1, l2, l3)):
        j = c ^ m

        @pl.when((j <= r) & (r - j < 3))
        def _():
            start(ref, rows.at[r - j], row_sems.at[r - j])

    for s, ref in enumerate((p0, p1, p2)):

        @pl.when(s <= r)
        def _():
            start(ref, panels.at[s], panel_sems.at[s])

    for s in range(3):

        @pl.when(s <= r)
        def _():
            wait(l0, rows.at[s], row_sems.at[s])
            wait(p0, panels.at[s], panel_sems.at[s])

            @pl.loop(0, acc_ref.shape[0] // TILE)
            def _(i):
                term = dot(rows[s, tile(i), :], panels[s])
                if s > 0:
                    term = term + acc_ref[tile(i), :]
                acc_ref[tile(i), :] = term


def product_end_kernel(l0, l1, l2, l3, acc_ref, p3_ref, *refs, deps, gated):
    below = refs[0]
    t_ref, tt_ref, sent_ref = refs[deps + gated : deps + gated + 3]
    block, block_sem, sem = refs[deps + 2 * gated + 3 :]
    r, c = position()
    half = below.at[sent_ref.shape[0] :]

    @pl.when((r == 1) | (r == 2))
    def _():
        start(half, sent_ref, sem)

    def finish(i, value):
        t_ref[tile(i), :] = value.astype(BF16)
        tt_ref[:, tile(i)] = value.T.astype(BF16)

    @pl.when(r < 3)
    def _():
        @pl.loop(0, acc_ref.shape[0] // TILE)
        def _(i):
            finish(i, acc_ref[tile(i), :])

    @pl.when(r == 3)
    def _():
        start_picked((l0, l1, l2, l3), c, block, block_sem)
        wait(l0, block, block_sem)

        @pl.loop(0, acc_ref.shape[0] // TILE)
        def _(i):
            finish(i, dot(block[tile(i), :], p3_ref[...]) + acc_ref[tile(i), :])

        @pl.loop(0, tt_ref.shape[0] // TILE)
        def _(i):
            sent_ref[tile(i), :] = dot(tt_ref[tile(i), :], block[...]).astype(BF16)

    @pl.when((r == 1) | (r == 2))
    def _():
        wait(half, sent_ref, sem)


def own_kernel(l0, l1, l2, l3, tt_ref, _in0, _in1, _in2, own_ref, _out0, _out1, _out2, block, sem):
    r, c = position()
    start_picked((l0, l1, l2, l3), r ^ c, block, sem)
    wait(l0, block, sem)

    @pl.loop(0, tt_ref.shape[0] // TILE)
    def _(i):
        own_ref[tile(i), :] = dot(tt_ref[tile(i), :], block[...])


def chain_kernel(l0, l1, l2, l3, tt_ref, came_ref, *refs, step, deps, gated):
    sent_ref = refs[deps + gated]
    block, sem = refs[deps + 2 * gated + 1 :]
    r, c = position()
    i = step + r - 3

    @pl.when(i >= 0)
    def _():
        start_picked((l0, l1, l2, l3), i ^ c, block, sem)
        wait(l0, block, sem)

        @pl.when(r == 3)
        def _():
            @pl.loop(0, tt_ref.shape[0] // TILE)
            def _(j):
                sent_ref[tile(j), :] = dot(tt_ref[tile(j), :], block[...]).astype(BF16)

        @pl.when(r < 3)
        def _():
            @pl.loop(0, tt_ref.shape[0] // TILE)
            def _(j):
                term = dot(tt_ref[tile(j), :], block[...])
                sent_ref[tile(j), :] = (term + came_ref[tile(j), :].astype(F32)).astype(BF16)

    @pl.when((i < 0) & (r == 1))
    def _():
        sent_ref[...] = came_ref[...]


def child_kernel(
    tt_ref, t_row_ref, child_ref, child_row_ref, _dep, far_ref, near_ref, onward_ref, own_ref, child_t
):
    r, _ = position()
    w = child_ref.shape[1]
    child_t[...] = child_ref[...].astype(F32).T.astype(BF16)
    for flip, ref in ((3, far_ref), (1, near_ref), (2, onward_ref), (0, own_ref)):
        columns = pl.ds(pl.multiple_of((r ^ flip) * w, w), w)

        @pl.loop(0, w // TILE)
        def _(i):
            term = dot(tt_ref[tile(i), :], t_row_ref[:, columns])
            term = term + dot(child_t[tile(i), :], child_row_ref[:, columns])
            ref[tile(i), :] = term.astype(ref.dtype)


def child_onward_kernel(own_ref, far_ref, _dep, out_ref):
    out_ref[...] = (own_ref[...] + far_ref[...].astype(F32)).astype(BF16)


def diagonal_kernel(l0, l1, l2, l3, _dep, acc_ref, left, held, sems):
    r, c = position()

    @pl.when(c <= r)
    def _():
        start_picked((l0, l1, l2, l3), r ^ c, left, sems.at[0])
        start(l0, held, sems.at[1])
        wait(l0, left, sems.at[0])
        wait(l0, held, sems.at[1])

        @pl.loop(0, acc_ref.shape[0] // TILE)
        def _(i):
            acc_ref[tile(i), :] = inner_dot(left[:, tile(i)], held[...])

    @pl.when(c > r)
    def _():
        acc_ref[...] = jnp.zeros_like(acc_ref)


def root_kernel(acc_ref, h1, h2, h3, b1, b2, b3, x1, x2, x3, f1, f2, f3, out_ref, acc, left, held, left_sems, held_sems):
    r, c = position()
    refs = ((h1, b1, x1, f1), (h2, b2, x2, f2), (h3, b3, x3, f3))
    needed = [(r + s < N) & (c <= r + s) for s in (1, 2, 3)]
    for s, places in enumerate(refs):

        @pl.when(needed[s])
        def _():
            start_picked(places, r ^ c, left.at[s], left_sems.at[s])
            start(places[0], held.at[s], held_sems.at[s])

    acc[...] = acc_ref[...]
    for s in range(3):

        @pl.when(needed[s])
        def _():
            wait(h1, left.at[s], left_sems.at[s])
            wait(h1, held.at[s], held_sems.at[s])

            @pl.loop(0, acc.shape[0] // TILE)
            def _(i):
                acc[tile(i), :] += inner_dot(left[s, :, tile(i)], held[s])

    out_ref[...] = acc[...].astype(BF16)


def cross_end_kernel(structure, own_ref, came_ref, _dep, out_ref):
    for b in range(own_ref.shape[1] // BLOCK):
        rows = slice(b * BLOCK, (b + 1) * BLOCK)
        total = own_ref[:, rows] + came_ref[:, rows].astype(F32)
        kept = structure[b] > 0
        out_ref[rows, :] = jnp.where(kept, -total.T, jnp.zeros_like(total.T)).astype(BF16)


def child_end_kernel(own_ref, near_ref, last_ref, _dep, out_ref):
    total = own_ref[...] + near_ref[...].astype(F32) + last_ref[...].astype(F32)
    out_ref[...] = total.T


ANY = pl.BlockSpec(memory_space=pl.ANY)
VMEM = pl.BlockSpec(memory_space=pltpu.VMEM)
SMEM = pl.BlockSpec(memory_space=pltpu.SMEM)


def local_call(kernel, in_specs, outs, scratch, *args, gated=0, out_specs=None):
    first = len(args) - gated
    outs = outs + [jax.ShapeDtypeStruct(x.shape, x.dtype) for x in args[first:]]
    return pl.pallas_call(
        kernel,
        out_shape=outs,
        in_specs=in_specs + [ANY] * (len(args) - len(in_specs)),
        out_specs=(out_specs or [VMEM] * (len(outs) - gated)) + [ANY] * gated,
        scratch_shapes=scratch,
        input_output_aliases={first + i: len(outs) - gated + i for i in range(gated)},
        compiler_params=pltpu.CompilerParams(vmem_limit_bytes=VMEM_BYTES),
        cost_estimate=pl.CostEstimate(flops=1, bytes_accessed=1, transcendentals=0),
    )(*args)


def together(*arrays, earlier=()):
    k = len(arrays)
    return pl.pallas_call(
        lambda *refs: None,
        out_shape=[jax.ShapeDtypeStruct(x.shape, x.dtype) for x in arrays],
        in_specs=[ANY] * (k + len(earlier)),
        out_specs=[ANY] * k,
        input_output_aliases={i: i for i in range(k)},
    )(*arrays, *earlier)


def square_plan(fields):
    n = N

    def move(x, target):
        pairs = []
        for f in range(fields):
            for r in range(n):
                for c in range(n):
                    to = target(r, c)
                    if to is not None and 0 <= to[0] < n:
                        pairs.append(((f * n + r) * n + c, (f * n + to[0]) * n + to[1]))
        return lax.ppermute(x, AXES, pairs)

    def up(x, s):
        return move(x, lambda r, c: (r + 1, c) if r >= s - 1 else None)

    def down(x, s):
        def target(r, c):
            k = r + s - 1
            return (r - 1, c) if k < n and c <= k else None

        return move(x, target)

    def on_device(root_inverse, child_inverse, panel, structure):
        h, w = panel.shape
        half = h // 2
        lower = lambda r, c: c <= r
        shape = jax.ShapeDtypeStruct
        dma = pltpu.SemaphoreType.DMA
        t_block, child_block = shape((w, h), BF16), shape((w, w), BF16)

        _, panel_kept = mask_panel(panel, structure)
        panel_1 = up(panel_kept, 1)
        root_across = move(root_inverse, lambda r, c: (r, c ^ 2) if lower(r, c) else None)
        below_1 = down(root_inverse, 1)
        (root_late,) = together(root_inverse, earlier=(panel_1,))
        root_beside = move(root_late, lambda r, c: (r, c ^ 1) if lower(r, c) else None)
        panel_2 = up(panel_1, 2)
        panel_2, child_late = together(
            panel_2, child_inverse, earlier=(below_1, root_across, root_beside)
        )
        child_row = lax.all_gather(child_late, "col", axis=1, tiled=True)
        panel_3 = up(panel_2, 3)
        root_both = move(root_across, lambda r, c: (r, c ^ 1) if lower(r, c ^ 2) else None)
        below_2a = down(below_1[:half], 2)
        across_3 = move(root_across, lambda r, c: (0, 2) if (r, c) == (3, 2) else None)

        def to_across(x, rows):
            return move(x, lambda r, c: (r, c ^ 2) if r == c and r in rows else None)

        def to_beside(x, rows):
            return move(x, lambda r, c: (r, c ^ 1) if r == c and r in rows else None)

        def on_beside(x, rows):
            return move(x, lambda r, c: (r, c ^ 1) if r == c ^ 2 and r in rows else None)

        across_1 = to_across(below_1, (1, 2))

        root_row = (root_inverse, root_beside, root_across, root_both)
        panels = (panel_kept, panel_1, panel_2, panel_3)
        (t_sum,) = local_call(
            product_kernel,
            [ANY] * 7,
            [shape((h, w), F32)],
            [pltpu.VMEM((3, h, h), BF16), pltpu.VMEM((3, h, w), BF16), dma((3,)), dma((3,))],
            *root_row,
            *panels[:3],
        )
        t, t_t, sent = local_call(
            functools.partial(product_end_kernel, deps=2, gated=0),
            [ANY] * 4 + [VMEM] * 2,
            [shape((h, w), BF16), t_block, t_block],
            [pltpu.VMEM((h, h), BF16), dma, dma],
            *root_row,
            t_sum,
            panel_3,
            below_1,
            across_1,
        )
        t_row = lax.all_gather(t, "col", axis=1, tiled=True)
        step = lambda x: move(x, lambda r, c: (r - 1, c))
        chain = [ANY] * 4 + [VMEM] * 2
        below_2b = came = move(sent, lambda r, c: (r - 1, c) if (r, c) != (1, 3) else None)
        far_1 = on_beside(across_1, (1, 2))
        own, below_1, below_2a, across_3 = local_call(
            own_kernel,
            [ANY] * 4 + [VMEM],
            [shape((w, h), F32)],
            [pltpu.VMEM((h, h), BF16), dma],
            *root_row,
            t_t,
            below_1,
            below_2a,
            across_3,
            gated=3,
        )
        far_3 = on_beside(across_3, (0,))
        below_3a = down(below_2a, 3)
        beside_1 = to_beside(below_1, (0, 1, 2))
        (sent,) = local_call(
            functools.partial(chain_kernel, step=1, deps=4, gated=0),
            chain,
            [t_block],
            [pltpu.VMEM((h, h), BF16), dma],
            *root_row,
            t_t,
            came,
            far_3,
            far_1,
            beside_1,
            below_3a,
        )
        below_2 = jnp.concatenate((below_2a, below_2b), 0)
        below_3b = came = step(sent)
        across_2 = to_across(below_2, (0, 1))
        beside_2 = to_beside(below_2, (0, 1))

        far_part, near_part, child_on, child_own = local_call(
            child_kernel,
            [VMEM] * 4,
            [child_block, child_block, shape((w, w), F32), shape((w, w), F32)],
            [pltpu.VMEM((w, w), BF16)],
            t_t,
            t_row,
            child_inverse,
            child_row,
            sent,
        )
        child_far = move(far_part, lambda r, c: (r ^ 1, c))
        child_near = move(near_part, lambda r, c: (r ^ 1, c))
        (root_sum,) = local_call(
            diagonal_kernel,
            [],
            [shape((h, h), F32)],
            [pltpu.VMEM((h, h), BF16), pltpu.VMEM((h, h), BF16), dma((2,))],
            *root_row,
            far_part,
        )
        sent, across_2, below_3a = local_call(
            functools.partial(chain_kernel, step=2, deps=3, gated=2),
            chain,
            [t_block],
            [pltpu.VMEM((h, h), BF16), dma],
            *root_row,
            t_t,
            came,
            child_far,
            child_near,
            beside_2,
            across_2,
            below_3a,
            gated=2,
        )
        came = step(sent)
        (child_onward,) = local_call(
            child_onward_kernel, [VMEM] * 2, [child_block], [], child_on, child_far, sent
        )
        child_last = move(child_onward, lambda r, c: (r ^ 2, c))
        below_3 = jnp.concatenate((below_3a, below_3b), 0)
        beside_3 = to_beside(below_3, (0,))
        far_2 = on_beside(across_2, (0, 1))
        (sigma_root,) = local_call(
            root_kernel,
            [VMEM],
            [shape((h, h), BF16)],
            [
                pltpu.VMEM((h, h), F32),
                pltpu.VMEM((3, h, h), BF16),
                pltpu.VMEM((3, h, h), BF16),
                dma((3,)),
                dma((3,)),
            ],
            root_sum,
            below_1,
            below_2,
            below_3,
            beside_1,
            beside_2,
            beside_3,
            across_1,
            across_2,
            across_3,
            far_1,
            far_2,
            far_3,
        )
        (sigma_cross,) = local_call(
            cross_end_kernel,
            [SMEM] + [VMEM] * 2,
            [shape((h, w), BF16)],
            [],
            structure,
            own,
            came,
            sigma_root,
        )
        (sigma_child,) = local_call(
            child_end_kernel,
            [VMEM] * 3,
            [shape((w, w), F32)],
            [],
            child_own,
            child_near,
            child_last,
            sigma_cross,
        )
        return (sigma_root, sigma_cross, sigma_child)

    return on_device


def solution(mesh):
    square = mesh.shape["row"] == N and mesh.shape["col"] == N
    spec = P(("fields", "row"), "col")
    return jax.shard_map(
        square_plan(mesh.shape["fields"]) if square else gather_plan,
        mesh=mesh,
        in_specs=(spec, spec, spec, P(("fields", "row"))),
        out_specs=(spec, spec, spec),
        check_vma=False,
    )
```
